32 devices in a mesh: groups: 2 (over x), frame: 16 (over z, y, core).
Axes of the slice: x: 2, y: 2, z: 4, core: 2. Of those that a mesh axis runs over, the one named last changes fastest.
Arguments:
- video_qkv: bfloat16 [3, 32, 128, 1536], P(None, ('groups', 'frame')), parts along dimension 1, may hold values from -8 to 8
- text_qkv: bfloat16 [3, 512, 1536], P(None, ('groups', 'frame')), parts along dimension 1, may hold values from -8 to 8
- head_kind: int32 [24], P('groups'), parts along dimension 0, may hold values from 0 to 1, as said below
- text_len: int32 [2], P('groups'), parts along dimension 0, may hold values from 64 to 256
Outputs:
- video_out: bfloat16 [32, 128, 1536], P(('groups', 'frame')), parts along dimension 0
- text_out: bfloat16 [512, 1536], P(('groups', 'frame')), parts along dimension 0
The draws below stay inside these ranges and needn't reach their ends.
There are 2 independent parts, one for each index of `groups`. The reference program is written for one: setup_inputs(seed, part) draws one part's arguments, and reference() takes and returns one part's arrays. A program takes and returns all parts, laid end to end along the dimension named above; each array names one. Nothing has to cross between parts.
Inputs may be any that keep to these rules, and one draw needn't show every extreme that they name: `head_kind`: exactly 6 of the 12 entries are 1.
All inputs are finite; a program needn't handle non-finite values.
Results may differ from the reference program's by a relative error of at most 0.009.
Values may be sent and summed in bfloat16 or wider, within the bound.
No kernel may reach another device: no remote copies, remote signals or barrier semaphores. Data moves between devices by JAX's collectives and lax.ppermute only.
A program may use at most 448 MiB of HBM per device.

```python
import jax
import jax.numpy as jnp
from jax import lax

H = 12
HD = 128
TXT = 256
P_SIZE = 128
FRAMES = 16
HT = 6


def rough_values(key, full_shape):
    base_key = jax.random.fold_in(key, 11)
    drawn = jnp.clip(jax.random.normal(base_key, full_shape, jnp.float32), -6.0, 6.0)
    return drawn


def draw_video_qkv(key, part):
    full_shape = (3, FRAMES, P_SIZE, H * HD)
    drawn = rough_values(jax.random.fold_in(key, 21), full_shape)
    return drawn.astype(jnp.bfloat16)


def draw_text_qkv(key, part):
    full_shape = (3, TXT, H * HD)
    drawn = rough_values(jax.random.fold_in(key, 31), full_shape)
    return drawn.astype(jnp.bfloat16)


def draw_head_kind(key, part):
    shuffled = jax.random.permutation(jax.random.fold_in(key, 3), H)
    return (shuffled < HT).astype(jnp.int32)


def setup_inputs(seed: int = 0, part: int = 0) -> dict:
    key_of = jax.random.split(jax.random.key(seed), 5)
    part_splits = jax.random.split(jax.random.fold_in(key_of[4], part), 5)
    video_qkv = draw_video_qkv(jax.random.fold_in(jax.random.fold_in(key_of[4], part), 71), part)
    text_qkv = draw_text_qkv(jax.random.fold_in(jax.random.fold_in(key_of[4], part), 71), part)
    head_kind = draw_head_kind(jax.random.fold_in(jax.random.fold_in(key_of[4], part), 71), part)
    text_len = jax.random.randint(part_splits[3], (1,), TXT // 4, TXT + 1).astype(jnp.int32)
    return {"video_qkv": video_qkv, "text_qkv": text_qkv, "head_kind": head_kind, "text_len": text_len}


masked_score = -1e30


def reference(video_qkv, text_qkv, head_kind, text_len):
    video = video_qkv.reshape(3, FRAMES, P_SIZE, H, HD)
    texts = text_qkv.reshape(3, TXT, H, HD)
    score_scale = HD ** -0.5
    text_valid = jnp.arange(TXT) < text_len[0]
    spatial_heads = jnp.nonzero(head_kind == 0, size=H - HT)[0].astype(jnp.int32)
    temporal_heads = jnp.nonzero(head_kind == 1, size=HT)[0].astype(jnp.int32)
    video_spatial = jnp.take(video, spatial_heads, axis=3)
    text_spatial = jnp.take(texts, spatial_heads, axis=2)
    text_keys_sp = text_spatial[1].astype(jnp.float32)
    text_values_sp = text_spatial[2].astype(jnp.float32)

    def spatial_frame(frame_block):
        queries = frame_block[0].astype(jnp.float32)
        own_scores = jnp.einsum("phd,khd->hpk", queries, frame_block[1].astype(jnp.float32)) * score_scale
        text_scores = jnp.einsum("phd,khd->hpk", queries, text_keys_sp) * score_scale
        text_scores = jnp.where(text_valid, text_scores, masked_score)
        row_max = jnp.maximum(own_scores.max(-1), text_scores.max(-1))[..., None]
        own_exp = jnp.exp(own_scores - row_max)
        text_exp = jnp.exp(text_scores - row_max)
        totals = own_exp.sum(-1) + text_exp.sum(-1)
        own_weight = lax.optimization_barrier(own_exp.astype(jnp.bfloat16)).astype(jnp.float32)
        text_weight = lax.optimization_barrier(text_exp.astype(jnp.bfloat16)).astype(jnp.float32)
        summed = jnp.einsum("hpk,khd->phd", own_weight, frame_block[2].astype(jnp.float32))
        summed = summed + jnp.einsum("hpk,khd->phd", text_weight, text_values_sp)
        return summed / totals.T[..., None]

    spatial_out = lax.map(spatial_frame, jnp.moveaxis(video_spatial, 1, 0))
    video_temporal = jnp.moveaxis(jnp.take(video, temporal_heads, axis=3), 3, 0)

    def temporal_head(head_block):
        queries = head_block[0].astype(jnp.float32)
        scores = jnp.einsum("fpd,gpd->pfg", queries, head_block[1].astype(jnp.float32)) * score_scale
        row_max = scores.max(-1, keepdims=True)
        exps = jnp.exp(scores - row_max)
        totals = exps.sum(-1)
        weight = lax.optimization_barrier(exps.astype(jnp.bfloat16)).astype(jnp.float32)
        summed = jnp.einsum("pfg,gpd->fpd", weight, head_block[2].astype(jnp.float32))
        return summed / totals.T[..., None]

    temporal_out = jnp.moveaxis(lax.map(temporal_head, video_temporal), 0, 2)
    joined = jnp.concatenate([spatial_out, temporal_out], axis=2)
    order = jnp.concatenate([spatial_heads, temporal_heads]).astype(jnp.int32)
    inverse = jnp.argsort(order).astype(jnp.int32)
    video_out = jnp.take(joined, inverse, axis=2).astype(jnp.bfloat16).reshape(FRAMES, P_SIZE, H * HD)

    flat_keys = video[1].reshape(FRAMES * P_SIZE, H, HD)
    flat_values = video[2].reshape(FRAMES * P_SIZE, H, HD)

    def text_head(head_index):
        queries = texts[0][:, head_index]
        text_scores = jnp.dot(queries, texts[1][:, head_index].T, preferred_element_type=jnp.float32) * score_scale
        text_scores = jnp.where(text_valid, text_scores, masked_score)
        video_scores = jnp.dot(queries, flat_keys[:, head_index].T, preferred_element_type=jnp.float32) * score_scale
        row_max = jnp.maximum(text_scores.max(-1), video_scores.max(-1))[:, None]
        text_exp = jnp.exp(text_scores - row_max)
        video_exp = jnp.exp(video_scores - row_max)
        totals = text_exp.sum(-1) + video_exp.sum(-1)
        summed = jnp.dot(text_exp.astype(jnp.bfloat16), texts[2][:, head_index], preferred_element_type=jnp.float32)
        summed = summed + jnp.dot(video_exp.astype(jnp.bfloat16), flat_values[:, head_index], preferred_element_type=jnp.float32)
        return summed / totals[:, None]

    text_all = lax.map(text_head, jnp.arange(H, dtype=jnp.int32))
    text_out = jnp.moveaxis(text_all, 0, 1).astype(jnp.bfloat16).reshape(TXT, H * HD)
    return video_out, text_out
```

```python
import functools

import jax
import jax.numpy as jnp
from jax import lax
from jax.experimental import pallas as pl
from jax.experimental.pallas import tpu as pltpu
from jax.sharding import PartitionSpec as P

masked_score = -1e30
lanes = 128


def contract_last(a, b):
    return lax.dot_general(a, b, (((1,), (1,)), ((), ())), preferred_element_type=jnp.float32)


def head_lanes(head):
    if isinstance(head, int):
        return pl.ds(head * lanes, lanes)
    return pl.ds(pl.multiple_of(head * lanes, lanes), lanes)


def list_heads(kind_ref, list_ref, head_count):
    ones = jnp.int32(0)
    for head in range(head_count):
        kind = kind_ref[head]
        slot = jnp.where(kind == 1, head_count + ones, head - ones)
        list_ref[slot] = jnp.int32(head)
        ones = ones + kind


def pack_kernel(head_count, kind_ref, video_ref, text_ref, temporal_ref, keys_ref, list_ref):
    list_heads(kind_ref, list_ref, head_count)
    half = head_count // 2
    for slot in range(half):
        head = list_ref[head_count + slot]
        for part in range(3):
            temporal_ref[:, pl.ds((part * half + slot) * lanes, lanes)] = video_ref[
                part, :, head_lanes(head)
            ]
    for slot in range(half):
        head = list_ref[slot]
        for part in range(2):
            keys_ref[:, pl.ds((part * half + slot) * lanes, lanes)] = text_ref[
                part + 1, :, head_lanes(head)
            ]


def temporal_kernel(half, stride, scale, block_ref, out_ref):
    rows = block_ref.shape[0]
    row = lax.broadcasted_iota(jnp.int32, (rows, rows), 0)
    column = lax.broadcasted_iota(jnp.int32, (rows, rows), 1)
    same = lax.rem(row, stride) == lax.rem(column, stride)
    for slot in range(half):
        query, key, value = (
            block_ref[:, pl.ds((part * half + slot) * lanes, lanes)] for part in range(3)
        )
        scores = jnp.where(same, contract_last(query, key) * scale, masked_score)
        exps = jnp.exp(scores - scores.max(-1, keepdims=True))
        total = exps.sum(-1, keepdims=True)
        summed = jnp.dot(exps.astype(jnp.bfloat16), value, preferred_element_type=jnp.float32)
        out_ref[:, pl.ds(slot * lanes, lanes)] = (summed / total).astype(jnp.bfloat16)


def spatial_kernel(
    head_count, shard, relative, scale, kind_ref, length_ref, video_ref, near_ref, far_ref, out_ref, list_ref
):
    list_heads(kind_ref, list_ref, head_count)
    half = head_count // 2
    positions = video_ref.shape[1]
    near = near_ref.shape[0]
    text_total = near + far_ref.shape[0]
    index = lax.broadcasted_iota(jnp.int32, (positions, text_total), 1)
    if relative:
        block = index // shard
        differs = (block & 3) * 4 + ((block >> 2) & 1) * 2 + ((block >> 3) & 1)
        index = (lax.axis_index("frame") ^ differs) * shard + lax.rem(index, shard)
    valid = index < length_ref[0]
    for slot in range(half):
        head = list_ref[slot]
        query, key, value = (video_ref[part, :, head_lanes(head)] for part in range(3))
        text_key, text_value = (
            jnp.concatenate(
                [
                    ref[:, pl.ds((part * half + slot) * lanes, lanes)]
                    for ref in (near_ref, far_ref)
                ],
                axis=0,
            )
            for part in range(2)
        )
        own_scores = contract_last(query, key) * scale
        text_scores = jnp.where(valid, contract_last(query, text_key) * scale, masked_score)
        row_max = jnp.maximum(
            own_scores.max(-1, keepdims=True), text_scores.max(-1, keepdims=True)
        )
        own_exp = jnp.exp(own_scores - row_max)
        text_exp = jnp.exp(text_scores - row_max)
        total = own_exp.sum(-1, keepdims=True) + text_exp.sum(-1, keepdims=True)
        summed = jnp.dot(own_exp.astype(jnp.bfloat16), value, preferred_element_type=jnp.float32)
        summed = summed + jnp.dot(
            text_exp.astype(jnp.bfloat16), text_value, preferred_element_type=jnp.float32
        )
        out_ref[:, pl.ds(slot * lanes, lanes)] = (summed / total).astype(jnp.bfloat16)


def text_kernel(
    head_count, shard, scale, length_ref, video_ref, other_ref, text_ref, other_text_ref, *refs
):
    query_refs, out_ref = refs[:-1], refs[-1]
    rows = out_ref.shape[0]
    me = lax.axis_index("frame")
    index = lax.broadcasted_iota(jnp.int32, (rows, shard), 1)
    valid = [index + owner * shard < length_ref[0] for owner in (me, me ^ 1)]
    lane = lax.broadcasted_iota(jnp.int32, (rows, lanes), 1)
    stats = jnp.zeros((rows, lanes), jnp.float32)
    for head in range(head_count):
        span = head_lanes(head)
        query = jnp.concatenate([ref[:, span] for ref in query_refs], axis=0)
        keys = [ref[1, :, span] for ref in (video_ref, other_ref, text_ref, other_text_ref)]
        values = [ref[2, :, span] for ref in (video_ref, other_ref, text_ref, other_text_ref)]
        scores = [contract_last(query, key) * scale for key in keys]
        scores = scores[:2] + [
            jnp.where(ok, score, masked_score) for ok, score in zip(valid, scores[2:])
        ]
        row_max = functools.reduce(
            jnp.maximum, [score.max(-1, keepdims=True) for score in scores]
        )
        point = row_max.astype(jnp.bfloat16).astype(jnp.float32)
        exps = [jnp.exp(score - point) for score in scores]
        total = sum(e.sum(-1, keepdims=True) for e in exps)
        summed = sum(
            jnp.dot(e.astype(jnp.bfloat16), value, preferred_element_type=jnp.float32)
            for e, value in zip(exps, values)
        )
        out_ref[:, span] = summed.astype(jnp.bfloat16)
        high = total.astype(jnp.bfloat16).astype(jnp.float32)
        for place, column in enumerate((point, high, total - high)):
            stats = jnp.where(lane == 3 * head + place, column, stats)
    out_ref[:, head_lanes(head_count)] = stats.astype(jnp.bfloat16)


def merge(head_count, blocks):
    stats = [block(head_count).astype(jnp.float32) for block in blocks]
    merged = []
    for head in range(head_count):
        points = [s[:, 3 * head : 3 * head + 1] for s in stats]
        totals = [s[:, 3 * head + 1 : 3 * head + 2] + s[:, 3 * head + 2 : 3 * head + 3] for s in stats]
        point = functools.reduce(jnp.maximum, points)
        factors = [jnp.exp(p - point) for p in points]
        total = sum(f * t for f, t in zip(factors, totals))
        summed = sum(f * block(head).astype(jnp.float32) for f, block in zip(factors, blocks))
        merged.append((point, total, summed))
    return merged


def reader(ref):
    return lambda head: ref[:, head_lanes(head)]


def merge_kernel(head_count, *refs):
    out_ref = refs[-1]
    lane = lax.broadcasted_iota(jnp.int32, (out_ref.shape[0], lanes), 1)
    stats = jnp.zeros(lane.shape, jnp.float32)
    for head, (point, total, summed) in enumerate(
        merge(head_count, [reader(ref) for ref in refs[:-1]])
    ):
        out_ref[:, head_lanes(head)] = summed.astype(jnp.bfloat16)
        high = total.astype(jnp.bfloat16).astype(jnp.float32)
        for place, column in enumerate((point, high, total - high)):
            stats = jnp.where(lane == 3 * head + place, column, stats)
    out_ref[:, head_lanes(head_count)] = stats.astype(jnp.bfloat16)


def finish_kernel(head_count, *refs):
    out_ref = refs[-1]
    for head, (_, total, summed) in enumerate(
        merge(head_count, [reader(ref) for ref in refs[:-1]])
    ):
        out_ref[:, head_lanes(head)] = (summed / total).astype(jnp.bfloat16)


def join_kernel(head_count, kind_ref, spatial_ref, temporal_ref, out_ref, list_ref):
    list_heads(kind_ref, list_ref, head_count)
    half = head_count // 2
    for kind, ref in enumerate((spatial_ref, temporal_ref)):
        for slot in range(half):
            out_ref[:, head_lanes(list_ref[kind * head_count + slot])] = ref[
                :, pl.ds(slot * lanes, lanes)
            ]


def call(kernel, name, out, scalars, arrays, list_size=0, flops=0):
    shapes = out if isinstance(out, list) else [out]
    outs = tuple(jax.ShapeDtypeStruct(shape, jnp.bfloat16) for shape in shapes)
    moved = sum(a.size * 2 for a in arrays) + sum(o.size * 2 for o in outs)
    result = pl.pallas_call(
        kernel,
        out_shape=outs,
        in_specs=[pl.BlockSpec(memory_space=pltpu.SMEM)] * len(scalars)
        + [pl.BlockSpec(memory_space=pltpu.VMEM)] * len(arrays),
        out_specs=tuple(pl.BlockSpec(memory_space=pltpu.VMEM) for _ in outs),
        scratch_shapes=[pltpu.SMEM((list_size,), jnp.int32)] if list_size else [],
        compiler_params=pltpu.CompilerParams(vmem_limit_bytes=24 * 2**20),
        cost_estimate=pl.CostEstimate(flops=flops, bytes_accessed=moved, transcendentals=0),
        name=name,
    )(*scalars, *arrays)
    return result if isinstance(out, list) else result[0]


def body(devices, video_qkv, text_qkv, head_kind, text_len):
    head_count = head_kind.shape[0]
    half = head_count // 2
    width = video_qkv.shape[-1]
    positions = video_qkv.shape[2]
    shard = text_qkv.shape[1]
    scale = (width // head_count) ** -0.5
    video = video_qkv.reshape(3, positions, width)
    relative = devices == 16

    def swap(array, bits):
        return lax.ppermute(array, "frame", [(i, i ^ bits) for i in range(devices)])

    temporal_block, spatial_keys = call(
        functools.partial(pack_kernel, head_count),
        "pack",
        [(positions, 3 * half * lanes), (shard, 2 * half * lanes)],
        [head_kind],
        [video, text_qkv],
        list_size=2 * head_count,
    )
    block = lax.all_to_all(temporal_block, "frame", split_axis=0, concat_axis=0, tiled=True)

    other_video = swap(video, 1)
    other_text = swap(text_qkv, 1)

    def attend(queries):
        rows = sum(q.shape[0] for q in queries)
        return call(
            functools.partial(text_kernel, head_count, shard, scale),
            "text",
            (rows, width + lanes),
            [text_len],
            [video, other_video, text_qkv, other_text, *queries],
            flops=8 * rows * width * (positions + shard),
        )

    queries = text_qkv[0]
    if relative:
        column = [queries] + [swap(queries, 4 * step) for step in (1, 2, 3)]
        across = swap(jnp.concatenate(column, axis=0), 2)
        sent = swap(attend([across]), 2)
        kept = attend(column)
        joined = call(
            functools.partial(merge_kernel, head_count), "merge", kept.shape, [], [kept, sent]
        )
        pieces = [joined[:shard]] + [
            swap(joined[step * shard : (step + 1) * shard], 4 * step) for step in (1, 2, 3)
        ]
        text_out = call(
            functools.partial(finish_kernel, head_count), "finish", (shard, width), [], pieces
        )
        keys_column = jnp.concatenate(
            [spatial_keys] + [swap(spatial_keys, 4 * step) for step in (1, 2, 3)], axis=0
        )
        near_keys = jnp.concatenate([keys_column, swap(keys_column, 2)], axis=0)
        far_keys = swap(near_keys, 1)
    else:
        side = [[2 * chip + core for chip in range(devices // 2)] for core in range(2)]
        gathered = lax.all_gather(queries, "frame", axis=0, tiled=True, axis_index_groups=side)
        partial_sums = lax.all_to_all(
            attend([gathered]), "frame", 0, 0, tiled=True, axis_index_groups=side
        ).reshape(devices // 2, shard, width + lanes)
        blocks = [
            lambda head, i=i: partial_sums[i, :, head * lanes : (head + 1) * lanes]
            for i in range(devices // 2)
        ]
        text_out = jnp.concatenate(
            [summed / total for _, total, summed in merge(head_count, blocks)], axis=1
        ).astype(jnp.bfloat16)
        all_keys = lax.all_gather(spatial_keys, "frame", axis=0, tiled=True)
        near_keys, far_keys = jnp.split(all_keys, 2, axis=0)

    spatial = call(
        functools.partial(spatial_kernel, head_count, shard, relative, scale),
        "spatial",
        (positions, half * lanes),
        [head_kind, text_len],
        [video, near_keys, far_keys],
        list_size=2 * head_count,
        flops=4 * positions * half * lanes * (positions + devices * shard),
    )
    result = call(
        functools.partial(temporal_kernel, half, positions // devices, scale),
        "temporal",
        (positions, half * lanes),
        [],
        [block],
        flops=4 * positions * half * lanes * positions,
    )
    temporal = lax.all_to_all(result, "frame", split_axis=0, concat_axis=0, tiled=True)
    video_out = call(
        functools.partial(join_kernel, head_count),
        "join",
        (positions, width),
        [head_kind],
        [spatial, temporal],
        list_size=2 * head_count,
    )
    return video_out.reshape(1, positions, width), text_out


def solution(mesh):
    in_specs = (
        P(None, ("groups", "frame"), None, None),
        P(None, ("groups", "frame"), None),
        P("groups"),
        P("groups"),
    )
    out_specs = (P(("groups", "frame"), None, None), P(("groups", "frame"), None))
    return jax.shard_map(
        functools.partial(body, mesh.shape["frame"]),
        mesh=mesh,
        in_specs=in_specs,
        out_specs=out_specs,
        check_vma=False,
    )
```

```python
import functools

import jax
import jax.numpy as jnp
from jax import lax
from jax.experimental import pallas as pl
from jax.experimental.pallas import tpu as pltpu
from jax.sharding import PartitionSpec as P

masked_score = -1e30
lanes = 128


def contract_last(a, b):
    return lax.dot_general(a, b, (((1,), (1,)), ((), ())), preferred_element_type=jnp.float32)


def head_lanes(head):
    if isinstance(head, int):
        return pl.ds(head * lanes, lanes)
    return pl.ds(pl.multiple_of(head * lanes, lanes), lanes)


def list_heads(kind_ref, list_ref, head_count):
    ones = jnp.int32(0)
    for head in range(head_count):
        kind = kind_ref[head]
        slot = jnp.where(kind == 1, head_count + ones, head - ones)
        list_ref[slot] = jnp.int32(head)
        ones = ones + kind


def pack_kernel(
    head_count, kind_ref, text_ref, video_ref, packed_ref, temporal_ref, list_ref, text_here, video_here, sems
):
    copies = [pltpu.make_async_copy(text_ref, text_here, sems.at[3])]
    for part in range(3):
        copies.append(
            pltpu.make_async_copy(video_ref.at[part], video_here.at[part], sems.at[part])
        )
    for copy in copies:
        copy.start()
    list_heads(kind_ref, list_ref, head_count)
    half = head_count // 2
    copies[0].wait()
    packed_ref[:, : head_count * lanes] = text_here[0]
    for slot in range(half):
        for part in range(2):
            packed_ref[:, head_lanes(head_count + part * half + slot)] = text_here[
                part + 1, :, head_lanes(list_ref[slot])
            ]
    for part in range(3):
        copies[part + 1].wait()
        for slot in range(half):
            temporal_ref[:, head_lanes(part * half + slot)] = video_here[
                part, :, head_lanes(list_ref[head_count + slot])
            ]


def temporal_kernel(half, stride, scale, block_ref, out_ref, score_ref, weight_ref):
    rows = block_ref.shape[0]
    row = lax.broadcasted_iota(jnp.int32, (rows, rows), 0)
    column = lax.broadcasted_iota(jnp.int32, (rows, rows), 1)
    same = lax.rem(row, stride) == lax.rem(column, stride)
    for slot in range(half):
        score_ref[slot] = contract_last(
            block_ref[:, head_lanes(slot)], block_ref[:, head_lanes(half + slot)]
        )
    totals = []
    for slot in range(half):
        scores = jnp.where(same, score_ref[slot] * scale, masked_score)
        exps = jnp.exp(scores - scores.max(-1, keepdims=True))
        totals.append(exps.sum(-1, keepdims=True))
        weight_ref[slot] = exps.astype(jnp.bfloat16)
    for slot in range(half):
        summed = jnp.dot(
            weight_ref[slot],
            block_ref[:, head_lanes(2 * half + slot)],
            preferred_element_type=jnp.float32,
        )
        out_ref[:, head_lanes(slot)] = (summed / totals[slot]).astype(jnp.bfloat16)


def spatial_kernel(
    head_count,
    shard,
    relative,
    scale,
    kind_ref,
    length_ref,
    video_ref,
    near_ref,
    far_ref,
    out_ref,
    list_ref,
    score_ref,
    weight_ref,
):
    list_heads(kind_ref, list_ref, head_count)
    half = head_count // 2
    positions = video_ref.shape[1]
    text_total = near_ref.shape[0] + far_ref.shape[0]
    index = lax.broadcasted_iota(jnp.int32, (8, text_total), 1)
    if relative:
        block = index // shard
        differs = (block & 3) * 4 + ((block >> 2) & 1) * 2 + ((block >> 3) & 1)
        index = (lax.axis_index("frame") ^ differs) * shard + lax.rem(index, shard)
    bias = jnp.where(index < length_ref[0], 0.0, masked_score)[:1]
    bias = jnp.concatenate([jnp.zeros((1, positions), jnp.float32), bias], axis=1)

    def gathered(part, slot):
        return jnp.concatenate(
            [
                video_ref[part + 1, :, head_lanes(list_ref[slot])],
                near_ref[:, head_lanes(part * half + slot)],
                far_ref[:, head_lanes(part * half + slot)],
            ],
            axis=0,
        )

    for slot in range(half):
        score_ref[slot] = contract_last(
            video_ref[0, :, head_lanes(list_ref[slot])], gathered(0, slot)
        )
    totals = []
    for slot in range(half):
        scores = score_ref[slot] * scale + bias
        exps = jnp.exp(scores - scores.max(-1, keepdims=True))
        totals.append(exps.sum(-1, keepdims=True))
        weight_ref[slot] = exps.astype(jnp.bfloat16)
    for slot in range(half):
        summed = jnp.dot(
            weight_ref[slot], gathered(1, slot), preferred_element_type=jnp.float32
        )
        out_ref[:, head_lanes(slot)] = (summed / totals[slot]).astype(jnp.bfloat16)


def text_kernel(head_count, shard, scale, length_ref, *refs):
    query_refs, key_refs = refs[:-7], refs[-7:-3]
    out_ref, score_ref, weight_ref = refs[-3:]
    rows = out_ref.shape[0]
    positions, text_rows = key_refs[0].shape[1], key_refs[2].shape[1]
    place = lax.broadcasted_iota(jnp.int32, (8, 2 * (positions + text_rows)), 1) - 2 * positions
    block = jnp.where(place >= text_rows, 1, 0)
    within = place - block * text_rows
    token = (lax.axis_index("frame") ^ block) * shard + within
    unused = (place >= 0) & ((within >= shard) | (token >= length_ref[0]))
    bias = jnp.where(unused, masked_score, 0.0)[:1]
    lane = lax.broadcasted_iota(jnp.int32, (rows, lanes), 1)
    stats = jnp.zeros((rows, lanes), jnp.float32)

    def gathered(part, head):
        return jnp.concatenate([ref[part, :, head_lanes(head)] for ref in key_refs], axis=0)

    for head in range(head_count):
        query = jnp.concatenate([ref[:, head_lanes(head)] for ref in query_refs], axis=0)
        score_ref[head] = contract_last(query, gathered(1, head))
    for head in range(head_count):
        scores = score_ref[head] * scale + bias
        point = scores.max(-1, keepdims=True).astype(jnp.bfloat16).astype(jnp.float32)
        exps = jnp.exp(scores - point)
        total = exps.sum(-1, keepdims=True)
        weight_ref[head] = exps.astype(jnp.bfloat16)
        high = total.astype(jnp.bfloat16).astype(jnp.float32)
        for place, column in enumerate((point, high, total - high)):
            stats = jnp.where(lane == 3 * head + place, column, stats)
    for head in range(head_count):
        summed = jnp.dot(
            weight_ref[head], gathered(2, head), preferred_element_type=jnp.float32
        )
        out_ref[:, head_lanes(head)] = summed.astype(jnp.bfloat16)
    out_ref[:, head_lanes(head_count)] = stats.astype(jnp.bfloat16)


def merge(head_count, blocks):
    stats = [block(head_count).astype(jnp.float32) for block in blocks]
    merged = []
    for head in range(head_count):
        points = [s[:, 3 * head : 3 * head + 1] for s in stats]
        totals = [s[:, 3 * head + 1 : 3 * head + 2] + s[:, 3 * head + 2 : 3 * head + 3] for s in stats]
        point = functools.reduce(jnp.maximum, points)
        factors = [jnp.exp(p - point) for p in points]
        total = sum(f * t for f, t in zip(factors, totals))
        summed = sum(f * block(head).astype(jnp.float32) for f, block in zip(factors, blocks))
        merged.append((point, total, summed))
    return merged


def reader(ref):
    return lambda head: ref[:, head_lanes(head)]


def merge_kernel(head_count, *refs):
    out_ref = refs[-1]
    lane = lax.broadcasted_iota(jnp.int32, (out_ref.shape[0], lanes), 1)
    stats = jnp.zeros(lane.shape, jnp.float32)
    for head, (point, total, summed) in enumerate(
        merge(head_count, [reader(ref) for ref in refs[:-1]])
    ):
        out_ref[:, head_lanes(head)] = summed.astype(jnp.bfloat16)
        high = total.astype(jnp.bfloat16).astype(jnp.float32)
        for place, column in enumerate((point, high, total - high)):
            stats = jnp.where(lane == 3 * head + place, column, stats)
    out_ref[:, head_lanes(head_count)] = stats.astype(jnp.bfloat16)


def finish_kernel(head_count, *refs):
    out_ref = refs[-1]
    for head, (_, total, summed) in enumerate(
        merge(head_count, [reader(ref) for ref in refs[:-1]])
    ):
        out_ref[:, head_lanes(head)] = (summed / total).astype(jnp.bfloat16)


def join_kernel(head_count, kind_ref, spatial_ref, temporal_ref, out_ref, list_ref):
    list_heads(kind_ref, list_ref, head_count)
    half = head_count // 2
    for kind, ref in enumerate((spatial_ref, temporal_ref)):
        for slot in range(half):
            out_ref[:, head_lanes(list_ref[kind * head_count + slot])] = ref[
                :, pl.ds(slot * lanes, lanes)
            ]


def after(array, *others):
    return lax.optimization_barrier((array, *others))[0]


def after(array, *others):
    return lax.optimization_barrier((array, *others))[0]


def call(kernel, name, out, scalars, arrays, scratch=(), flops=0, space=pltpu.VMEM):
    outs = [jax.ShapeDtypeStruct(shape, jnp.bfloat16) for shape in out]
    moved = sum(a.size * 2 for a in arrays) + sum(o.size * 2 for o in outs)
    return pl.pallas_call(
        kernel,
        out_shape=outs,
        in_specs=[pl.BlockSpec(memory_space=pltpu.SMEM)] * len(scalars)
        + [pl.BlockSpec(memory_space=space)] * len(arrays),
        out_specs=[pl.BlockSpec(memory_space=pltpu.VMEM)] * len(outs),
        scratch_shapes=scratch,
        compiler_params=pltpu.CompilerParams(vmem_limit_bytes=32 * 2**20),
        cost_estimate=pl.CostEstimate(flops=flops, bytes_accessed=moved, transcendentals=0),
        name=name,
    )(*scalars, *arrays)


def score_scratch(heads, rows, keys):
    return [pltpu.VMEM((heads, rows, keys), jnp.float32), pltpu.VMEM((heads, rows, keys), jnp.bfloat16)]


def body(devices, video_qkv, text_qkv, head_kind, text_len):
    head_count = head_kind.shape[0]
    half = head_count // 2
    width = video_qkv.shape[-1]
    positions = video_qkv.shape[2]
    shard = text_qkv.shape[1]
    scale = (width // head_count) ** -0.5
    video = video_qkv.reshape(3, positions, width)
    relative = devices == 16
    head_list = [pltpu.SMEM((2 * head_count,), jnp.int32)]

    def swap(array, bits):
        return lax.ppermute(array, "frame", [(i, i ^ bits) for i in range(devices)])

    packed_text, packed_video = call(
        functools.partial(pack_kernel, head_count),
        "pack",
        [(shard, 2 * width), (positions, 3 * half * lanes)],
        [head_kind],
        [text_qkv, video],
        head_list
        + [pltpu.VMEM(a.shape, a.dtype) for a in (text_qkv, video)]
        + [pltpu.SemaphoreType.DMA((4,))],
        space=pl.ANY,
    )
    block = lax.all_to_all(packed_video, "frame", split_axis=0, concat_axis=0, tiled=True)

    text_rows = -(-shard // 16) * 16
    text = jnp.pad(text_qkv, ((0, 0), (0, text_rows - shard), (0, 0)))
    keys = [video, swap(video, 1), text, swap(text, 1)]

    def attend(queries):
        rows = sum(q.shape[0] for q in queries)
        key_count = 2 * (positions + text_rows)
        return call(
            functools.partial(text_kernel, head_count, shard, scale),
            "text",
            [(rows, width + lanes)],
            [text_len],
            [*queries, *keys],
            score_scratch(head_count, rows, key_count),
            flops=4 * rows * width * key_count,
        )[0]

    if relative:
        column = [packed_text] + [swap(packed_text, 4 * step) for step in (1, 2, 3)]
        across = swap(jnp.concatenate([c[:, :width] for c in column], axis=0), 2)
        kept = attend(column)
        across = after(across, kept)
        partial_sums = attend([across])
        sent = swap(partial_sums, 2)
        block = after(block, partial_sums)
        (joined,) = call(
            functools.partial(merge_kernel, head_count), "merge", [kept.shape], [], [kept, sent]
        )
        pieces = [joined[:shard]] + [
            swap(joined[step * shard : (step + 1) * shard], 4 * step) for step in (1, 2, 3)
        ]
        keys_column = jnp.concatenate([c[:, width:] for c in column], axis=0)
        keys_column = after(keys_column, partial_sums)
        near_keys = jnp.concatenate([keys_column, swap(keys_column, 2)], axis=0)
        far_keys = swap(near_keys, 1)
    else:
        side = [[2 * chip + core for chip in range(devices // 2)] for core in range(2)]
        gathered = lax.all_gather(
            packed_text[:, :width], "frame", axis=0, tiled=True, axis_index_groups=side
        )
        partial_sums = lax.all_to_all(
            attend([gathered]), "frame", 0, 0, tiled=True, axis_index_groups=side
        ).reshape(devices // 2, shard, width + lanes)
        blocks = [
            lambda head, i=i: partial_sums[i, :, head * lanes : (head + 1) * lanes]
            for i in range(devices // 2)
        ]
        text_out = jnp.concatenate(
            [summed / total for _, total, summed in merge(head_count, blocks)], axis=1
        ).astype(jnp.bfloat16)
        all_keys = lax.all_gather(packed_text[:, width:], "frame", axis=0, tiled=True)
        near_keys, far_keys = jnp.split(all_keys, 2, axis=0)

    key_count = positions + devices * shard
    (spatial,) = call(
        functools.partial(spatial_kernel, head_count, shard, relative, scale),
        "spatial",
        [(positions, half * lanes)],
        [head_kind, text_len],
        [video, near_keys, far_keys],
        head_list + score_scratch(half, positions, key_count),
        flops=4 * positions * half * lanes * key_count,
    )
    if relative:
        pieces[0] = after(pieces[0], spatial)
        (text_out,) = call(
            functools.partial(finish_kernel, head_count), "finish", [(shard, width)], [], pieces
        )
    (result,) = call(
        functools.partial(temporal_kernel, half, positions // devices, scale),
        "temporal",
        [(positions, half * lanes)],
        [],
        [block],
        score_scratch(half, positions, positions),
        flops=4 * positions * half * lanes * positions,
    )
    temporal = lax.all_to_all(result, "frame", split_axis=0, concat_axis=0, tiled=True)
    (video_out,) = call(
        functools.partial(join_kernel, head_count),
        "join",
        [(positions, width)],
        [head_kind],
        [spatial, temporal],
        head_list,
    )
    return video_out.reshape(1, positions, width), text_out


def solution(mesh):
    in_specs = (
        P(None, ("groups", "frame"), None, None),
        P(None, ("groups", "frame"), None),
        P("groups"),
        P("groups"),
    )
    out_specs = (P(("groups", "frame"), None, None), P(("groups", "frame"), None))
    return jax.shard_map(
        functools.partial(body, mesh.shape["frame"]),
        mesh=mesh,
        in_specs=in_specs,
        out_specs=out_specs,
        check_vma=False,
    )
```

```python
import functools

import jax
import jax.numpy as jnp
from jax import lax
from jax.experimental import pallas as pl
from jax.experimental.pallas import tpu as pltpu
from jax.sharding import PartitionSpec as P

masked_score = -1e30
lanes = 128


def contract_last(a, b):
    return lax.dot_general(a, b, (((1,), (1,)), ((), ())), preferred_element_type=jnp.float32)


def head_lanes(head):
    if isinstance(head, int):
        return pl.ds(head * lanes, lanes)
    return pl.ds(pl.multiple_of(head * lanes, lanes), lanes)


def list_heads(kind_ref, list_ref, head_count):
    ones = jnp.int32(0)
    for head in range(head_count):
        kind = kind_ref[head]
        slot = jnp.where(kind == 1, head_count + ones, head - ones)
        list_ref[slot] = jnp.int32(head)
        ones = ones + kind


def pack_kernel(
    head_count,
    kind_ref,
    text_ref,
    video_ref,
    packed_ref,
    temporal_ref,
    list_ref,
    kind_here,
    text_here,
    video_here,
    packed_here,
    temporal_here,
    in_sems,
    out_sems,
):
    half = head_count // 2
    width = head_count * lanes
    copies = [
        pltpu.make_async_copy(kind_ref, kind_here, in_sems.at[0]),
        pltpu.make_async_copy(text_ref, text_here, in_sems.at[1]),
    ]
    for part in range(3):
        copies.append(
            pltpu.make_async_copy(video_ref.at[part], video_here.at[part], in_sems.at[part + 2])
        )
    for copy in copies:
        copy.start()
    copies[0].wait()
    list_heads(kind_here, list_ref, head_count)
    copies[1].wait()
    packed_here[:, :width] = text_here[0]
    for slot in range(half):
        for part in range(2):
            packed_here[:, head_lanes(head_count + part * half + slot)] = text_here[
                part + 1, :, head_lanes(list_ref[slot])
            ]
    sends = [pltpu.make_async_copy(packed_here, packed_ref, out_sems.at[0])]
    sends[0].start()
    for part in range(3):
        copies[part + 2].wait()
        for slot in range(half):
            temporal_here[:, head_lanes(part * half + slot)] = video_here[
                part, :, head_lanes(list_ref[head_count + slot])
            ]
        span = pl.ds(part * half * lanes, half * lanes)
        sends.append(
            pltpu.make_async_copy(
                temporal_here.at[:, span], temporal_ref.at[:, span], out_sems.at[part + 1]
            )
        )
        sends[-1].start()
    for send in sends:
        send.wait()


def stack_kernel(*refs):
    for half, out_ref in enumerate(refs[-2:]):
        width = out_ref.shape[1]
        out_ref[...] = jnp.concatenate(
            [ref[:, pl.ds(half * width, width)] for ref in refs[:-2]], axis=0
        )


def temporal_kernel(half, stride, scale, block_ref, out_ref, score_ref, weight_ref):
    rows = block_ref.shape[0]
    row = lax.broadcasted_iota(jnp.int32, (rows, rows), 0)
    column = lax.broadcasted_iota(jnp.int32, (rows, rows), 1)
    same = lax.rem(row, stride) == lax.rem(column, stride)
    for slot in range(half):
        score_ref[slot] = contract_last(
            block_ref[:, head_lanes(slot)], block_ref[:, head_lanes(half + slot)]
        )
    totals = []
    for slot in range(half):
        scores = jnp.where(same, score_ref[slot] * scale, masked_score)
        exps = jnp.exp(scores - scores.max(-1, keepdims=True))
        totals.append(exps.sum(-1, keepdims=True))
        weight_ref[slot] = exps.astype(jnp.bfloat16)
    for slot in range(half):
        summed = jnp.dot(
            weight_ref[slot],
            block_ref[:, head_lanes(2 * half + slot)],
            preferred_element_type=jnp.float32,
        )
        out_ref[:, head_lanes(slot)] = (summed / totals[slot]).astype(jnp.bfloat16)


def spatial_kernel(
    head_count,
    shard,
    relative,
    scale,
    kind_ref,
    length_ref,
    video_ref,
    *refs,
):
    text_refs = refs[:-4]
    out_ref, list_ref, score_ref, weight_ref = refs[-4:]
    list_heads(kind_ref, list_ref, head_count)
    half = head_count // 2
    positions = video_ref.shape[1]
    text_total = sum(ref.shape[0] for ref in text_refs)
    index = lax.broadcasted_iota(jnp.int32, (8, text_total), 1)
    if relative:
        block = index // shard
        differs = (block & 3) * 4 + ((block >> 2) & 1) * 2 + ((block >> 3) & 1)
        index = (lax.axis_index("frame") ^ differs) * shard + lax.rem(index, shard)
    bias = jnp.where(index < length_ref[0], 0.0, masked_score)[:1]
    bias = jnp.concatenate([jnp.zeros((1, positions), jnp.float32), bias], axis=1)

    def gathered(part, slot):
        return jnp.concatenate(
            [video_ref[part + 1, :, head_lanes(list_ref[slot])]]
            + [ref[:, head_lanes(part * half + slot)] for ref in text_refs],
            axis=0,
        )

    for slot in range(half):
        score_ref[slot] = contract_last(
            video_ref[0, :, head_lanes(list_ref[slot])], gathered(0, slot)
        )
    totals = []
    for slot in range(half):
        scores = score_ref[slot] * scale + bias
        exps = jnp.exp(scores - scores.max(-1, keepdims=True))
        totals.append(exps.sum(-1, keepdims=True))
        weight_ref[slot] = exps.astype(jnp.bfloat16)
    for slot in range(half):
        summed = jnp.dot(
            weight_ref[slot], gathered(1, slot), preferred_element_type=jnp.float32
        )
        out_ref[:, head_lanes(slot)] = (summed / totals[slot]).astype(jnp.bfloat16)


def text_kernel(head_count, shard, scale, length_ref, *refs):
    query_refs, key_refs = refs[:-7], refs[-7:-3]
    out_ref, score_ref, weight_ref = refs[-3:]
    rows = out_ref.shape[0]
    positions, text_rows = key_refs[0].shape[1], key_refs[2].shape[1]
    place = lax.broadcasted_iota(jnp.int32, (8, 2 * (positions + text_rows)), 1) - 2 * positions
    block = jnp.where(place >= text_rows, 1, 0)
    within = place - block * text_rows
    token = (lax.axis_index("frame") ^ block) * shard + within
    unused = (place >= 0) & ((within >= shard) | (token >= length_ref[0]))
    bias = jnp.where(unused, masked_score, 0.0)[:1]
    lane = lax.broadcasted_iota(jnp.int32, (rows, lanes), 1)
    stats = jnp.zeros((rows, lanes), jnp.float32)

    def gathered(part, head):
        return jnp.concatenate([ref[part, :, head_lanes(head)] for ref in key_refs], axis=0)

    for head in range(head_count):
        query = jnp.concatenate([ref[:, head_lanes(head)] for ref in query_refs], axis=0)
        score_ref[head] = contract_last(query, gathered(1, head))
    for head in range(head_count):
        scores = score_ref[head] * scale + bias
        point = scores.max(-1, keepdims=True).astype(jnp.bfloat16).astype(jnp.float32)
        exps = jnp.exp(scores - point)
        total = exps.sum(-1, keepdims=True)
        weight_ref[head] = exps.astype(jnp.bfloat16)
        high = total.astype(jnp.bfloat16).astype(jnp.float32)
        for place, column in enumerate((point, high, total - high)):
            stats = jnp.where(lane == 3 * head + place, column, stats)
    for head in range(head_count):
        summed = jnp.dot(
            weight_ref[head], gathered(2, head), preferred_element_type=jnp.float32
        )
        out_ref[:, head_lanes(head)] = summed.astype(jnp.bfloat16)
    out_ref[:, head_lanes(head_count)] = stats.astype(jnp.bfloat16)


def merge(head_count, blocks):
    stats = [block(head_count).astype(jnp.float32) for block in blocks]
    merged = []
    for head in range(head_count):
        points = [s[:, 3 * head : 3 * head + 1] for s in stats]
        totals = [s[:, 3 * head + 1 : 3 * head + 2] + s[:, 3 * head + 2 : 3 * head + 3] for s in stats]
        point = functools.reduce(jnp.maximum, points)
        factors = [jnp.exp(p - point) for p in points]
        total = sum(f * t for f, t in zip(factors, totals))
        summed = sum(f * block(head).astype(jnp.float32) for f, block in zip(factors, blocks))
        merged.append((point, total, summed))
    return merged


def reader(ref):
    return lambda head: ref[:, head_lanes(head)]


def merge_kernel(head_count, *refs):
    out_ref = refs[-1]
    lane = lax.broadcasted_iota(jnp.int32, (out_ref.shape[0], lanes), 1)
    stats = jnp.zeros(lane.shape, jnp.float32)
    for head, (point, total, summed) in enumerate(
        merge(head_count, [reader(ref) for ref in refs[:-1]])
    ):
        out_ref[:, head_lanes(head)] = summed.astype(jnp.bfloat16)
        high = total.astype(jnp.bfloat16).astype(jnp.float32)
        for place, column in enumerate((point, high, total - high)):
            stats = jnp.where(lane == 3 * head + place, column, stats)
    out_ref[:, head_lanes(head_count)] = stats.astype(jnp.bfloat16)


def finish_kernel(head_count, *refs):
    out_ref = refs[-1]
    for head, (_, total, summed) in enumerate(
        merge(head_count, [reader(ref) for ref in refs[:-1]])
    ):
        out_ref[:, head_lanes(head)] = (summed / total).astype(jnp.bfloat16)


def join_kernel(head_count, kind_ref, spatial_ref, temporal_ref, out_ref, list_ref):
    list_heads(kind_ref, list_ref, head_count)
    half = head_count // 2
    for kind, ref in enumerate((spatial_ref, temporal_ref)):
        for slot in range(half):
            out_ref[:, head_lanes(list_ref[kind * head_count + slot])] = ref[
                :, pl.ds(slot * lanes, lanes)
            ]


def after(array, *others):
    return lax.optimization_barrier((array, *others))[0]


def after(array, *others):
    return lax.optimization_barrier((array, *others))[0]


def call(kernel, name, out, scalars, arrays, scratch=(), flops=0, space=pltpu.VMEM, out_space=pltpu.VMEM, limit=32):
    outs = [jax.ShapeDtypeStruct(shape, jnp.bfloat16) for shape in out]
    moved = sum(a.size * 2 for a in arrays) + sum(o.size * 2 for o in outs)
    return pl.pallas_call(
        kernel,
        out_shape=outs,
        in_specs=[pl.BlockSpec(memory_space=pltpu.SMEM)] * len(scalars)
        + [pl.BlockSpec(memory_space=space)] * len(arrays),
        out_specs=[pl.BlockSpec(memory_space=out_space)] * len(outs),
        scratch_shapes=scratch,
        compiler_params=pltpu.CompilerParams(vmem_limit_bytes=limit * 2**20),
        cost_estimate=pl.CostEstimate(flops=flops, bytes_accessed=moved, transcendentals=0),
        name=name,
    )(*scalars, *arrays)


def score_scratch(heads, rows, keys):
    return [pltpu.VMEM((heads, rows, keys), jnp.float32), pltpu.VMEM((heads, rows, keys), jnp.bfloat16)]


def body(devices, video_qkv, text_qkv, head_kind, text_len):
    head_count = head_kind.shape[0]
    half = head_count // 2
    width = video_qkv.shape[-1]
    positions = video_qkv.shape[2]
    shard = text_qkv.shape[1]
    scale = (width // head_count) ** -0.5
    video = video_qkv.reshape(3, positions, width)
    relative = devices == 16
    head_list = [pltpu.SMEM((2 * head_count,), jnp.int32)]

    def swap(array, bits):
        return lax.ppermute(array, "frame", [(i, i ^ bits) for i in range(devices)])

    packed_text, packed_video = call(
        functools.partial(pack_kernel, head_count),
        "pack",
        [(shard, 2 * width), (positions, 3 * half * lanes)],
        [],
        [head_kind, text_qkv, video],
        head_list
        + [pltpu.SMEM(head_kind.shape, jnp.int32)]
        + [pltpu.VMEM(a.shape, a.dtype) for a in (text_qkv, video)]
        + [pltpu.VMEM((shard, 2 * width), jnp.bfloat16)]
        + [pltpu.VMEM((positions, 3 * half * lanes), jnp.bfloat16)]
        + [pltpu.SemaphoreType.DMA((5,)), pltpu.SemaphoreType.DMA((4,))],
        space=pl.ANY,
        out_space=pl.ANY,
        limit=60,
    )
    block = lax.all_to_all(packed_video, "frame", split_axis=0, concat_axis=0, tiled=True)

    text_rows = -(-shard // 16) * 16
    text = jnp.pad(text_qkv, ((0, 0), (0, text_rows - shard), (0, 0)))
    other_text = swap(text, 1)
    keys = [video, swap(video, 1), text, other_text]

    def attend(queries):
        rows = sum(q.shape[0] for q in queries)
        key_count = 2 * (positions + text_rows)
        return call(
            functools.partial(text_kernel, head_count, shard, scale),
            "text",
            [(rows, width + lanes)],
            [text_len],
            [*queries, *keys],
            score_scratch(head_count, rows, key_count),
            flops=4 * rows * width * key_count,
        )[0]

    def attend_temporal(received):
        return call(
            functools.partial(temporal_kernel, half, positions // devices, scale),
            "temporal",
            [(positions, half * lanes)],
            [],
            [received],
            score_scratch(half, positions, positions),
            flops=4 * positions * half * lanes * positions,
        )

    if relative:
        column = [packed_text] + [swap(packed_text, 4 * step) for step in (1, 2, 3)]
        queries_column, keys_column = call(
            stack_kernel, "stack", [(4 * shard, width)] * 2, [], column, flops=20000000000
        )
        across = swap(queries_column, 2)
        kept = attend([queries_column])
        across = after(across, kept)
        partial_sums = attend([across])
        sent = swap(partial_sums, 2)
        (result,) = attend_temporal(after(block, partial_sums))
        sent = after(sent, result)
        (joined,) = call(
            functools.partial(merge_kernel, head_count), "merge", [kept.shape], [], [kept, sent]
        )
        pieces = [joined[:shard]] + [
            swap(joined[step * shard : (step + 1) * shard], 4 * step) for step in (1, 2, 3)
        ]
        across_keys = swap(after(keys_column, result), 2)
        across_keys = after(across_keys, joined)
        text_keys = [keys_column, across_keys, swap(keys_column, 1), swap(across_keys, 1)]
    else:
        (result,) = attend_temporal(block)
        side = [[2 * chip + core for chip in range(devices // 2)] for core in range(2)]
        gathered = lax.all_gather(
            packed_text[:, :width], "frame", axis=0, tiled=True, axis_index_groups=side
        )
        partial_sums = lax.all_to_all(
            attend([gathered]), "frame", 0, 0, tiled=True, axis_index_groups=side
        ).reshape(devices // 2, shard, width + lanes)
        blocks = [
            lambda head, i=i: partial_sums[i, :, head * lanes : (head + 1) * lanes]
            for i in range(devices // 2)
        ]
        text_out = jnp.concatenate(
            [summed / total for _, total, summed in merge(head_count, blocks)], axis=1
        ).astype(jnp.bfloat16)
        all_keys = lax.all_gather(packed_text[:, width:], "frame", axis=0, tiled=True)
        text_keys = [all_keys]

    key_count = positions + devices * shard
    (spatial,) = call(
        functools.partial(spatial_kernel, head_count, shard, relative, scale),
        "spatial",
        [(positions, half * lanes)],
        [head_kind, text_len],
        [video, *text_keys],
        head_list + score_scratch(half, positions, key_count),
        flops=4 * positions * half * lanes * key_count,
    )
    if relative:
        pieces[0] = after(pieces[0], spatial)
        (text_out,) = call(
            functools.partial(finish_kernel, head_count), "finish", [(shard, width)], [], pieces
        )
    temporal = lax.all_to_all(result, "frame", split_axis=0, concat_axis=0, tiled=True)
    (video_out,) = call(
        functools.partial(join_kernel, head_count),
        "join",
        [(positions, width)],
        [head_kind],
        [spatial, temporal],
        head_list,
    )
    return video_out.reshape(1, positions, width), text_out


def solution(mesh):
    in_specs = (
        P(None, ("groups", "frame"), None, None),
        P(None, ("groups", "frame"), None),
        P("groups"),
        P("groups"),
    )
    out_specs = (P(("groups", "frame"), None, None), P(("groups", "frame"), None))
    return jax.shard_map(
        functools.partial(body, mesh.shape["frame"]),
        mesh=mesh,
        in_specs=in_specs,
        out_specs=out_specs,
        check_vma=False,
    )
```

```python
import functools

import jax
import jax.numpy as jnp
from jax import lax
from jax.experimental import pallas as pl
from jax.experimental.pallas import tpu as pltpu
from jax.sharding import PartitionSpec as P

masked_score = -1e30
lanes = 128
stat_lanes = 32


def contract_last(a, b):
    return lax.dot_general(a, b, (((1,), (1,)), ((), ())), preferred_element_type=jnp.float32)


def head_lanes(head):
    if isinstance(head, int):
        return pl.ds(head * lanes, lanes)
    return pl.ds(pl.multiple_of(head * lanes, lanes), lanes)


def list_heads(kind_ref, list_ref, head_count):
    ones = jnp.int32(0)
    for head in range(head_count):
        kind = kind_ref[head]
        slot = jnp.where(kind == 1, head_count + ones, head - ones)
        list_ref[slot] = jnp.int32(head)
        ones = ones + kind


def pack_kernel(
    head_count,
    kind_ref,
    text_ref,
    video_ref,
    packed_ref,
    temporal_ref,
    list_ref,
    kind_here,
    text_here,
    video_here,
    packed_here,
    temporal_here,
    in_sems,
    out_sems,
):
    half = head_count // 2
    width = head_count * lanes
    copies = [
        pltpu.make_async_copy(kind_ref, kind_here, in_sems.at[0]),
        pltpu.make_async_copy(text_ref, text_here, in_sems.at[1]),
    ]
    for part in range(3):
        copies.append(
            pltpu.make_async_copy(video_ref.at[part], video_here.at[part], in_sems.at[part + 2])
        )
    for copy in copies:
        copy.start()
    copies[0].wait()
    list_heads(kind_here, list_ref, head_count)
    copies[1].wait()
    packed_here[:, :width] = text_here[0]
    for slot in range(half):
        for part in range(2):
            packed_here[:, head_lanes(head_count + part * half + slot)] = text_here[
                part + 1, :, head_lanes(list_ref[slot])
            ]
    sends = [pltpu.make_async_copy(packed_here, packed_ref, out_sems.at[0])]
    sends[0].start()
    for part in range(3):
        copies[part + 2].wait()
        for slot in range(half):
            temporal_here[:, head_lanes(part * half + slot)] = video_here[
                part, :, head_lanes(list_ref[head_count + slot])
            ]
        span = pl.ds(part * half * lanes, half * lanes)
        sends.append(
            pltpu.make_async_copy(
                temporal_here.at[:, span], temporal_ref.at[:, span], out_sems.at[part + 1]
            )
        )
        sends[-1].start()
    for send in sends:
        send.wait()


def stack_kernel(*refs):
    for half, out_ref in enumerate(refs[-2:]):
        width = out_ref.shape[1]
        out_ref[...] = jnp.concatenate(
            [ref[:, pl.ds(half * width, width)] for ref in refs[:-2]], axis=0
        )


def temporal_kernel(half, stride, scale, block_ref, out_ref, score_ref, weight_ref, here_ref, sems):
    rows = block_ref.shape[0]
    row = lax.broadcasted_iota(jnp.int32, (rows, rows), 0)
    column = lax.broadcasted_iota(jnp.int32, (rows, rows), 1)
    same = lax.rem(row, stride) == lax.rem(column, stride)
    for slot in range(half):
        score_ref[slot] = contract_last(
            block_ref[:, head_lanes(slot)], block_ref[:, head_lanes(half + slot)]
        )
    totals = []
    for slot in range(half):
        scores = jnp.where(same, score_ref[slot] * scale, masked_score)
        exps = jnp.exp(scores - scores.max(-1, keepdims=True))
        totals.append(exps.sum(-1, keepdims=True))
        weight_ref[slot] = exps.astype(jnp.bfloat16)
    sends = []
    for slot in range(half):
        summed = jnp.dot(
            weight_ref[slot],
            block_ref[:, head_lanes(2 * half + slot)],
            preferred_element_type=jnp.float32,
        )
        here_ref[:, head_lanes(slot)] = (summed / totals[slot]).astype(jnp.bfloat16)
        if slot % 2 == 1 or slot == half - 1:
            span = pl.ds((slot // 2) * 2 * lanes, (slot % 2 + 1) * lanes)
            sends.append(
                pltpu.make_async_copy(here_ref.at[:, span], out_ref.at[:, span], sems.at[slot // 2])
            )
            sends[-1].start()
    for send in sends:
        send.wait()


def spatial_kernel(
    head_count,
    shard,
    relative,
    scale,
    blocks,
    kind_ref,
    length_ref,
    video_ref,
    *refs,
):
    text_refs = refs[:blocks]
    out_ref, list_ref, keys_ref, score_ref, weight_ref, sems = refs[blocks:]
    width = keys_ref.shape[1]
    copies = []
    rows = 0
    for i, ref in enumerate(text_refs):
        source = ref.at[:, pl.ds(ref.shape[1] - width, width)]
        target = keys_ref.at[pl.ds(rows, ref.shape[0])]
        copies.append(pltpu.make_async_copy(source, target, sems.at[i]))
        copies[-1].start()
        rows += ref.shape[0]
    list_heads(kind_ref, list_ref, head_count)
    half = head_count // 2
    positions = video_ref.shape[1]
    index = lax.broadcasted_iota(jnp.int32, (8, rows), 1)
    if relative:
        block = index // shard
        differs = (block & 3) * 4 + ((block >> 2) & 1) * 2 + ((block >> 3) & 1)
        index = (lax.axis_index("frame") ^ differs) * shard + lax.rem(index, shard)
    bias = jnp.where(index < length_ref[0], 0.0, masked_score)[:1]
    bias = jnp.concatenate([jnp.zeros((1, positions), jnp.float32), bias], axis=1)

    def gathered(part, slot):
        return jnp.concatenate(
            [
                video_ref[part + 1, :, head_lanes(list_ref[slot])],
                keys_ref[:, head_lanes(part * half + slot)],
            ],
            axis=0,
        )

    for copy in copies:
        copy.wait()
    for slot in range(half):
        score_ref[slot] = contract_last(
            video_ref[0, :, head_lanes(list_ref[slot])], gathered(0, slot)
        )
    totals = []
    for slot in range(half):
        scores = score_ref[slot] * scale + bias
        exps = jnp.exp(scores - scores.max(-1, keepdims=True))
        totals.append(exps.sum(-1, keepdims=True))
        weight_ref[slot] = exps.astype(jnp.bfloat16)
    for slot in range(half):
        summed = jnp.dot(
            weight_ref[slot], gathered(1, slot), preferred_element_type=jnp.float32
        )
        out_ref[:, head_lanes(slot)] = (summed / totals[slot]).astype(jnp.bfloat16)


def text_kernel(head_count, shard, scale, length_ref, *refs):
    query_ref, key_refs, rider_refs = refs[0], refs[1:5], refs[5:-3]
    out_ref, score_ref, weight_ref = refs[-3:]
    rows = out_ref.shape[0]
    positions, text_rows = key_refs[0].shape[1], key_refs[2].shape[1]
    place = lax.broadcasted_iota(jnp.int32, (8, 2 * (positions + text_rows)), 1) - 2 * positions
    block = jnp.where(place >= text_rows, 1, 0)
    within = place - block * text_rows
    token = (lax.axis_index("frame") ^ block) * shard + within
    unused = (place >= 0) & ((within >= shard) | (token >= length_ref[0]))
    bias = jnp.where(unused, masked_score, 0.0)[:1]
    lane = lax.broadcasted_iota(jnp.int32, (rows, lanes), 1)
    stats = jnp.zeros((rows, lanes), jnp.float32)

    def gathered(part, head):
        return jnp.concatenate([ref[part, :, head_lanes(head)] for ref in key_refs], axis=0)

    for head in range(head_count):
        score_ref[head] = contract_last(query_ref[:, head_lanes(head)], gathered(1, head))
    for head in range(head_count):
        scores = score_ref[head] * scale + bias
        point = scores.max(-1, keepdims=True).astype(jnp.bfloat16).astype(jnp.float32)
        exps = jnp.exp(scores - point)
        total = exps.sum(-1, keepdims=True)
        weight_ref[head] = exps.astype(jnp.bfloat16)
        high = total.astype(jnp.bfloat16).astype(jnp.float32)
        for place, column in enumerate((point, high, total - high)):
            stats = jnp.where(lane == place * stat_lanes + head, column, stats)
    for head in range(head_count):
        summed = jnp.dot(
            weight_ref[head], gathered(2, head), preferred_element_type=jnp.float32
        )
        out_ref[:, head_lanes(head)] = summed.astype(jnp.bfloat16)
    out_ref[:, head_lanes(head_count)] = stats.astype(jnp.bfloat16)
    for ref in rider_refs:
        out_ref[:, pl.ds((head_count + 1) * lanes, ref.shape[1])] = ref[...]


def merge(head_count, blocks):
    stats = [block(head_count).astype(jnp.float32) for block in blocks]
    points, highs, lows = (
        [s[:, part * stat_lanes : (part + 1) * stat_lanes] for s in stats] for part in range(3)
    )
    point = functools.reduce(jnp.maximum, points)
    factors = [jnp.exp(p - point) for p in points]
    total = sum(f * (high + low) for f, high, low in zip(factors, highs, lows))
    return point, total, factors


def weigh(head, factors, blocks):
    return sum(
        f[:, head : head + 1] * block(head).astype(jnp.float32)
        for f, block in zip(factors, blocks)
    )


def reader(ref):
    return lambda head: ref[:, head_lanes(head)]


def merge_kernel(head_count, parts, first_ref, second_ref, *out_refs):
    blocks = [reader(first_ref), reader(second_ref)]
    point, total, factors = merge(head_count, blocks)
    high = total.astype(jnp.bfloat16).astype(jnp.float32)

    def store(head, merged):
        for ref, places in zip(out_refs, parts):
            ref[:, head_lanes(head)] = jnp.concatenate(
                [merged[i * 16 : (i + 1) * 16] for i in places], axis=0
            ).astype(jnp.bfloat16)

    for head in range(head_count):
        store(head, weigh(head, factors, blocks))
    store(head_count, jnp.concatenate([point, high, total - high, jnp.zeros_like(point)], axis=1))


def finish_kernel(head_count, *refs):
    out_ref = refs[-1]
    blocks = [reader(ref) for ref in refs[:-1]]
    _, total, factors = merge(head_count, blocks)
    total = jnp.where(total > 0, total, 1.0)
    factors = [f / total for f in factors]
    for head in range(head_count):
        out_ref[:, head_lanes(head)] = weigh(head, factors, blocks).astype(jnp.bfloat16)


def join_kernel(head_count, kind_ref, spatial_ref, temporal_ref, out_ref, list_ref):
    list_heads(kind_ref, list_ref, head_count)
    half = head_count // 2
    for kind, ref in enumerate((spatial_ref, temporal_ref)):
        for slot in range(half):
            out_ref[:, head_lanes(list_ref[kind * head_count + slot])] = ref[
                :, pl.ds(slot * lanes, lanes)
            ]


def after(array, *others):
    return lax.optimization_barrier((array, *others))[0]


def after(array, *others):
    return lax.optimization_barrier((array, *others))[0]


def call(kernel, name, out, scalars, arrays, scratch=(), flops=0, spaces=None, out_space=pltpu.VMEM, limit=32):
    outs = [jax.ShapeDtypeStruct(shape, jnp.bfloat16) for shape in out]
    moved = sum(a.size * 2 for a in arrays) + sum(o.size * 2 for o in outs)
    return pl.pallas_call(
        kernel,
        out_shape=outs,
        in_specs=[pl.BlockSpec(memory_space=pltpu.SMEM)] * len(scalars)
        + [pl.BlockSpec(memory_space=m) for m in spaces or [pltpu.VMEM] * len(arrays)],
        out_specs=[pl.BlockSpec(memory_space=out_space)] * len(outs),
        scratch_shapes=scratch,
        compiler_params=pltpu.CompilerParams(vmem_limit_bytes=limit * 2**20),
        cost_estimate=pl.CostEstimate(flops=flops, bytes_accessed=moved, transcendentals=0),
        name=name,
    )(*scalars, *arrays)


def score_scratch(heads, rows, keys):
    return [pltpu.VMEM((heads, rows, keys), jnp.float32), pltpu.VMEM((heads, rows, keys), jnp.bfloat16)]


def body(devices, video_qkv, text_qkv, head_kind, text_len):
    head_count = head_kind.shape[0]
    half = head_count // 2
    width = video_qkv.shape[-1]
    positions = video_qkv.shape[2]
    shard = text_qkv.shape[1]
    scale = (width // head_count) ** -0.5
    video = video_qkv.reshape(3, positions, width)
    relative = devices == 16
    head_list = [pltpu.SMEM((2 * head_count,), jnp.int32)]

    def swap(array, bits):
        return lax.ppermute(array, "frame", [(i, i ^ bits) for i in range(devices)])

    packed_text, packed_video = call(
        functools.partial(pack_kernel, head_count),
        "pack",
        [(shard, 2 * width), (positions, 3 * half * lanes)],
        [],
        [head_kind, text_qkv, video],
        head_list
        + [pltpu.SMEM(head_kind.shape, jnp.int32)]
        + [pltpu.VMEM(a.shape, a.dtype) for a in (text_qkv, video)]
        + [pltpu.VMEM((shard, 2 * width), jnp.bfloat16)]
        + [pltpu.VMEM((positions, 3 * half * lanes), jnp.bfloat16)]
        + [pltpu.SemaphoreType.DMA((5,)), pltpu.SemaphoreType.DMA((4,))],
        spaces=[pl.ANY] * 3,
        out_space=pl.ANY,
        limit=60,
    )
    block = lax.all_to_all(packed_video, "frame", split_axis=0, concat_axis=0, tiled=True)

    text_rows = -(-shard // 16) * 16
    text = jnp.pad(text_qkv, ((0, 0), (0, text_rows - shard), (0, 0)))
    other_text = swap(text, 1)
    keys = [video, swap(video, 1), text, other_text]

    def attend(queries, riders=()):
        rows = queries.shape[0]
        key_count = 2 * (positions + text_rows)
        return call(
            functools.partial(text_kernel, head_count, shard, scale),
            "text",
            [(rows, width + lanes + sum(r.shape[1] for r in riders))],
            [text_len],
            [queries, *keys, *riders],
            score_scratch(head_count, rows, key_count),
            flops=4 * rows * width * key_count,
        )[0]

    def attend_temporal(received):
        return call(
            functools.partial(temporal_kernel, half, positions // devices, scale),
            "temporal",
            [(positions, half * lanes)],
            [],
            [received],
            score_scratch(half, positions, positions)
            + [pltpu.VMEM((positions, half * lanes), jnp.bfloat16)]
            + [pltpu.SemaphoreType.DMA((-(-half // 2),))],
            flops=4 * positions * half * lanes * positions,
            out_space=pl.ANY,
        )

    if relative:
        column = [packed_text] + [swap(packed_text, 4 * step) for step in (1, 2, 3)]
        queries_column, keys_column = call(
            stack_kernel, "stack", [(4 * shard, width)] * 2, [], column, flops=8 * 10**9
        )
        across = swap(queries_column, 2)
        kept = attend(queries_column)
        across = after(across, kept)
        partial_sums = attend(across, [keys_column])
        sent = swap(partial_sums, 2)
        (result,) = attend_temporal(after(block, partial_sums))
        sent = after(sent, result)
        joined = call(
            functools.partial(merge_kernel, head_count, ((0,), (1,), (2,), (3,))),
            "merge",
            [(shard, width + lanes)] * 4,
            [],
            [kept, sent],
            flops=20 * 10**9,
        )
        pieces = [joined[0]] + [swap(joined[step], 4 * step) for step in (1, 2, 3)]
        text_keys = [keys_column, sent, swap(keys_column, 1), swap(sent, 1)]
    else:
        (result,) = attend_temporal(block)
        side = [[2 * chip + core for chip in range(devices // 2)] for core in range(2)]
        gathered = lax.all_gather(
            packed_text[:, :width], "frame", axis=0, tiled=True, axis_index_groups=side
        )
        partial_sums = lax.all_to_all(
            attend(gathered), "frame", 0, 0, tiled=True, axis_index_groups=side
        ).reshape(devices // 2, shard, width + lanes)
        blocks = [
            lambda head, i=i: partial_sums[i, :, head * lanes : (head + 1) * lanes]
            for i in range(devices // 2)
        ]
        _, total, factors = merge(head_count, blocks)
        text_out = jnp.concatenate(
            [
                weigh(head, factors, blocks) / total[:, head : head + 1]
                for head in range(head_count)
            ],
            axis=1,
        ).astype(jnp.bfloat16)
        all_keys = lax.all_gather(packed_text[:, width:], "frame", axis=0, tiled=True)
        text_keys = [all_keys]

    key_count = positions + devices * shard
    (spatial,) = call(
        functools.partial(spatial_kernel, head_count, shard, relative, scale, len(text_keys)),
        "spatial",
        [(positions, half * lanes)],
        [head_kind, text_len],
        [video, *text_keys],
        head_list
        + [pltpu.VMEM((key_count - positions, 2 * half * lanes), jnp.bfloat16)]
        + score_scratch(half, positions, key_count)
        + [pltpu.SemaphoreType.DMA((len(text_keys),))],
        flops=4 * positions * half * lanes * key_count,
        spaces=[pltpu.VMEM] + [pl.ANY] * len(text_keys),
    )
    if relative:
        pieces[0] = after(pieces[0], spatial)
        (text_out,) = call(
            functools.partial(finish_kernel, head_count), "finish", [(shard, width)], [], pieces
        )
    temporal = lax.all_to_all(result, "frame", split_axis=0, concat_axis=0, tiled=True)
    (video_out,) = call(
        functools.partial(join_kernel, head_count),
        "join",
        [(positions, width)],
        [head_kind],
        [spatial, temporal],
        head_list,
    )
    return video_out.reshape(1, positions, width), text_out


def solution(mesh):
    in_specs = (
        P(None, ("groups", "frame"), None, None),
        P(None, ("groups", "frame"), None),
        P("groups"),
        P("groups"),
    )
    out_specs = (P(("groups", "frame"), None, None), P(("groups", "frame"), None))
    return jax.shard_map(
        functools.partial(body, mesh.shape["frame"]),
        mesh=mesh,
        in_specs=in_specs,
        out_specs=out_specs,
        check_vma=False,
    )
```

```python
import functools

import jax
import jax.numpy as jnp
from jax import lax
from jax.experimental import pallas as pl
from jax.experimental.pallas import tpu as pltpu
from jax.sharding import PartitionSpec as P

masked_score = -1e30
lanes = 128
stat_lanes = 32


def contract_last(a, b):
    return lax.dot_general(a, b, (((1,), (1,)), ((), ())), preferred_element_type=jnp.float32)


def head_lanes(head):
    if isinstance(head, int):
        return pl.ds(head * lanes, lanes)
    return pl.ds(pl.multiple_of(head * lanes, lanes), lanes)


def list_heads(kind_ref, list_ref, head_count):
    ones = jnp.int32(0)
    for head in range(head_count):
        kind = kind_ref[head]
        slot = jnp.where(kind == 1, head_count + ones, head - ones)
        list_ref[slot] = jnp.int32(head)
        ones = ones + kind


def pack_kernel(
    head_count,
    kind_ref,
    text_ref,
    video_ref,
    packed_ref,
    temporal_ref,
    list_ref,
    kind_here,
    text_here,
    video_here,
    packed_here,
    temporal_here,
    in_sems,
    out_sems,
):
    half = head_count // 2
    width = head_count * lanes
    copies = [
        pltpu.make_async_copy(kind_ref, kind_here, in_sems.at[0]),
        pltpu.make_async_copy(text_ref, text_here, in_sems.at[1]),
    ]
    for part in range(3):
        copies.append(
            pltpu.make_async_copy(video_ref.at[part], video_here.at[part], in_sems.at[part + 2])
        )
    for copy in copies:
        copy.start()
    copies[0].wait()
    list_heads(kind_here, list_ref, head_count)
    copies[1].wait()
    packed_here[:, :width] = text_here[0]
    for slot in range(half):
        for part in range(2):
            packed_here[:, head_lanes(head_count + part * half + slot)] = text_here[
                part + 1, :, head_lanes(list_ref[slot])
            ]
    sends = [pltpu.make_async_copy(packed_here, packed_ref, out_sems.at[0])]
    sends[0].start()
    for part in range(3):
        copies[part + 2].wait()
        for slot in range(half):
            temporal_here[:, head_lanes(part * half + slot)] = video_here[
                part, :, head_lanes(list_ref[head_count + slot])
            ]
        span = pl.ds(part * half * lanes, half * lanes)
        sends.append(
            pltpu.make_async_copy(
                temporal_here.at[:, span], temporal_ref.at[:, span], out_sems.at[part + 1]
            )
        )
        sends[-1].start()
    for send in sends:
        send.wait()


def stack_kernel(*refs):
    for half, out_ref in enumerate(refs[-2:]):
        width = out_ref.shape[1]
        out_ref[...] = jnp.concatenate(
            [ref[:, pl.ds(half * width, width)] for ref in refs[:-2]], axis=0
        )


def temporal_kernel(half, stride, scale, block_ref, out_ref, score_ref, weight_ref, here_ref, sems):
    rows = block_ref.shape[0]
    row = lax.broadcasted_iota(jnp.int32, (rows, rows), 0)
    column = lax.broadcasted_iota(jnp.int32, (rows, rows), 1)
    same = lax.rem(row, stride) == lax.rem(column, stride)
    for slot in range(half):
        score_ref[slot] = contract_last(
            block_ref[:, head_lanes(slot)], block_ref[:, head_lanes(half + slot)]
        )
    totals = []
    for slot in range(half):
        scores = jnp.where(same, score_ref[slot] * scale, masked_score)
        exps = jnp.exp(scores - scores.max(-1, keepdims=True))
        totals.append(exps.sum(-1, keepdims=True))
        weight_ref[slot] = exps.astype(jnp.bfloat16)
    sends = []
    for slot in range(half):
        summed = jnp.dot(
            weight_ref[slot],
            block_ref[:, head_lanes(2 * half + slot)],
            preferred_element_type=jnp.float32,
        )
        here_ref[:, head_lanes(slot)] = (summed / totals[slot]).astype(jnp.bfloat16)
        if slot % 2 == 1 or slot == half - 1:
            span = pl.ds((slot // 2) * 2 * lanes, (slot % 2 + 1) * lanes)
            sends.append(
                pltpu.make_async_copy(here_ref.at[:, span], out_ref.at[:, span], sems.at[slot // 2])
            )
            sends[-1].start()
    for send in sends:
        send.wait()


def spatial_kernel(
    head_count,
    shard,
    relative,
    scale,
    kind_ref,
    length_ref,
    video_ref,
    *refs,
):
    text_refs = refs[:-4]
    out_ref, list_ref, score_ref, weight_ref = refs[-4:]
    list_heads(kind_ref, list_ref, head_count)
    half = head_count // 2
    positions = video_ref.shape[1]
    text_total = sum(ref.shape[0] for ref in text_refs)
    index = lax.broadcasted_iota(jnp.int32, (8, text_total), 1)
    if relative:
        block = index // shard
        differs = (block & 3) * 4 + ((block >> 2) & 1) * 2 + ((block >> 3) & 1)
        index = (lax.axis_index("frame") ^ differs) * shard + lax.rem(index, shard)
    bias = jnp.where(index < length_ref[0], 0.0, masked_score)[:1]
    bias = jnp.concatenate([jnp.zeros((1, positions), jnp.float32), bias], axis=1)

    def gathered(part, slot):
        return jnp.concatenate(
            [video_ref[part + 1, :, head_lanes(list_ref[slot])]]
            + [
                ref[:, head_lanes(ref.shape[1] // lanes + (part - 2) * half + slot)]
                for ref in text_refs
            ],
            axis=0,
        )

    for slot in range(half):
        score_ref[slot] = contract_last(
            video_ref[0, :, head_lanes(list_ref[slot])], gathered(0, slot)
        )
    totals = []
    for slot in range(half):
        scores = score_ref[slot] * scale + bias
        exps = jnp.exp(scores - scores.max(-1, keepdims=True))
        totals.append(exps.sum(-1, keepdims=True))
        weight_ref[slot] = exps.astype(jnp.bfloat16)
    for slot in range(half):
        summed = jnp.dot(
            weight_ref[slot], gathered(1, slot), preferred_element_type=jnp.float32
        )
        out_ref[:, head_lanes(slot)] = (summed / totals[slot]).astype(jnp.bfloat16)


def text_kernel(head_count, shard, scale, length_ref, *refs):
    query_ref, key_refs, rider_refs = refs[0], refs[1:5], refs[5:-3]
    out_ref, score_ref, weight_ref = refs[-3:]
    rows = out_ref.shape[0]
    positions, text_rows = key_refs[0].shape[1], key_refs[2].shape[1]
    place = lax.broadcasted_iota(jnp.int32, (8, 2 * (positions + text_rows)), 1) - 2 * positions
    block = jnp.where(place >= text_rows, 1, 0)
    within = place - block * text_rows
    token = (lax.axis_index("frame") ^ block) * shard + within
    unused = (place >= 0) & ((within >= shard) | (token >= length_ref[0]))
    bias = jnp.where(unused, masked_score, 0.0)[:1]
    lane = lax.broadcasted_iota(jnp.int32, (rows, lanes), 1)
    stats = jnp.zeros((rows, lanes), jnp.float32)

    def gathered(part, head):
        return jnp.concatenate([ref[part, :, head_lanes(head)] for ref in key_refs], axis=0)

    for head in range(head_count):
        score_ref[head] = contract_last(query_ref[:, head_lanes(head)], gathered(1, head))
    for head in range(head_count):
        scores = score_ref[head] * scale + bias
        point = scores.max(-1, keepdims=True).astype(jnp.bfloat16).astype(jnp.float32)
        exps = jnp.exp(scores - point)
        total = exps.sum(-1, keepdims=True)
        weight_ref[head] = exps.astype(jnp.bfloat16)
        high = total.astype(jnp.bfloat16).astype(jnp.float32)
        for place, column in enumerate((point, high, total - high)):
            stats = jnp.where(lane == place * stat_lanes + head, column, stats)
    for head in range(head_count):
        summed = jnp.dot(
            weight_ref[head], gathered(2, head), preferred_element_type=jnp.float32
        )
        out_ref[:, head_lanes(head)] = summed.astype(jnp.bfloat16)
    out_ref[:, head_lanes(head_count)] = stats.astype(jnp.bfloat16)
    for ref in rider_refs:
        out_ref[:, pl.ds((head_count + 1) * lanes, ref.shape[1])] = ref[...]


def merge(head_count, blocks):
    stats = [block(head_count).astype(jnp.float32) for block in blocks]
    points, highs, lows = (
        [s[:, part * stat_lanes : (part + 1) * stat_lanes] for s in stats] for part in range(3)
    )
    point = functools.reduce(jnp.maximum, points)
    factors = [jnp.exp(p - point) for p in points]
    total = sum(f * (high + low) for f, high, low in zip(factors, highs, lows))
    return point, total, factors


def weigh(head, factors, blocks):
    return sum(
        f[:, head : head + 1] * block(head).astype(jnp.float32)
        for f, block in zip(factors, blocks)
    )


def reader(ref):
    return lambda head: ref[:, head_lanes(head)]


def merge_kernel(head_count, parts, first_ref, second_ref, *out_refs):
    blocks = [reader(first_ref), reader(second_ref)]
    point, total, factors = merge(head_count, blocks)
    high = total.astype(jnp.bfloat16).astype(jnp.float32)

    def store(head, merged):
        for ref, places in zip(out_refs, parts):
            ref[:, head_lanes(head)] = jnp.concatenate(
                [merged[i * 16 : (i + 1) * 16] for i in places], axis=0
            ).astype(jnp.bfloat16)

    for head in range(head_count):
        store(head, weigh(head, factors, blocks))
    store(head_count, jnp.concatenate([point, high, total - high, jnp.zeros_like(point)], axis=1))


def finish_kernel(head_count, *refs):
    out_ref, here_ref, sems = refs[-3:]
    blocks = [reader(ref) for ref in refs[:-3]]
    _, total, factors = merge(head_count, blocks)
    total = jnp.where(total > 0, total, 1.0)
    factors = [f / total for f in factors]
    half = head_count // 2
    sends = []
    for part in range(2):
        for head in range(part * half, (part + 1) * half):
            here_ref[:, head_lanes(head)] = weigh(head, factors, blocks).astype(jnp.bfloat16)
        span = pl.ds(part * half * lanes, half * lanes)
        sends.append(
            pltpu.make_async_copy(here_ref.at[:, span], out_ref.at[:, span], sems.at[part])
        )
        sends[-1].start()
    for send in sends:
        send.wait()


def join_kernel(head_count, kind_ref, spatial_ref, temporal_ref, out_ref, list_ref):
    list_heads(kind_ref, list_ref, head_count)
    half = head_count // 2
    for kind, ref in enumerate((spatial_ref, temporal_ref)):
        for slot in range(half):
            out_ref[:, head_lanes(list_ref[kind * head_count + slot])] = ref[
                :, pl.ds(slot * lanes, lanes)
            ]


def after(array, *others):
    return lax.optimization_barrier((array, *others))[0]


def after(array, *others):
    return lax.optimization_barrier((array, *others))[0]


def call(kernel, name, out, scalars, arrays, scratch=(), flops=0, space=pltpu.VMEM, out_space=pltpu.VMEM, limit=32):
    outs = [jax.ShapeDtypeStruct(shape, jnp.bfloat16) for shape in out]
    moved = sum(a.size * 2 for a in arrays) + sum(o.size * 2 for o in outs)
    return pl.pallas_call(
        kernel,
        out_shape=outs,
        in_specs=[pl.BlockSpec(memory_space=pltpu.SMEM)] * len(scalars)
        + [pl.BlockSpec(memory_space=space)] * len(arrays),
        out_specs=[pl.BlockSpec(memory_space=out_space)] * len(outs),
        scratch_shapes=scratch,
        compiler_params=pltpu.CompilerParams(vmem_limit_bytes=limit * 2**20),
        cost_estimate=pl.CostEstimate(flops=flops, bytes_accessed=moved, transcendentals=0),
        name=name,
    )(*scalars, *arrays)


def score_scratch(heads, rows, keys):
    return [pltpu.VMEM((heads, rows, keys), jnp.float32), pltpu.VMEM((heads, rows, keys), jnp.bfloat16)]


def body(devices, video_qkv, text_qkv, head_kind, text_len):
    head_count = head_kind.shape[0]
    half = head_count // 2
    width = video_qkv.shape[-1]
    positions = video_qkv.shape[2]
    shard = text_qkv.shape[1]
    scale = (width // head_count) ** -0.5
    video = video_qkv.reshape(3, positions, width)
    relative = devices == 16
    head_list = [pltpu.SMEM((2 * head_count,), jnp.int32)]

    def swap(array, bits):
        return lax.ppermute(array, "frame", [(i, i ^ bits) for i in range(devices)])

    packed_text, packed_video = call(
        functools.partial(pack_kernel, head_count),
        "pack",
        [(shard, 2 * width), (positions, 3 * half * lanes)],
        [],
        [head_kind, text_qkv, video],
        head_list
        + [pltpu.SMEM(head_kind.shape, jnp.int32)]
        + [pltpu.VMEM(a.shape, a.dtype) for a in (text_qkv, video)]
        + [pltpu.VMEM((shard, 2 * width), jnp.bfloat16)]
        + [pltpu.VMEM((positions, 3 * half * lanes), jnp.bfloat16)]
        + [pltpu.SemaphoreType.DMA((5,)), pltpu.SemaphoreType.DMA((4,))],
        space=pl.ANY,
        out_space=pl.ANY,
        limit=60,
    )
    block = lax.all_to_all(packed_video, "frame", split_axis=0, concat_axis=0, tiled=True)

    text_rows = -(-shard // 16) * 16
    text = jnp.pad(text_qkv, ((0, 0), (0, text_rows - shard), (0, 0)))
    other_text = swap(text, 1)
    keys = [video, swap(video, 1), text, other_text]

    def attend(queries, riders=()):
        rows = queries.shape[0]
        key_count = 2 * (positions + text_rows)
        return call(
            functools.partial(text_kernel, head_count, shard, scale),
            "text",
            [(rows, width + lanes + sum(r.shape[1] for r in riders))],
            [text_len],
            [queries, *keys, *riders],
            score_scratch(head_count, rows, key_count),
            flops=4 * rows * width * key_count,
        )[0]

    def attend_temporal(received):
        return call(
            functools.partial(temporal_kernel, half, positions // devices, scale),
            "temporal",
            [(positions, half * lanes)],
            [],
            [received],
            score_scratch(half, positions, positions)
            + [pltpu.VMEM((positions, half * lanes), jnp.bfloat16)]
            + [pltpu.SemaphoreType.DMA((-(-half // 2),))],
            flops=4 * positions * half * lanes * positions,
            out_space=pl.ANY,
        )

    if relative:
        column = [packed_text] + [swap(packed_text, 4 * step) for step in (1, 2, 3)]
        queries_column, keys_column = call(
            stack_kernel, "stack", [(4 * shard, width)] * 2, [], column, flops=8 * 10**9
        )
        across = swap(queries_column, 2)
        kept = attend(queries_column)
        across = after(across, kept)
        partial_sums = attend(across, [keys_column])
        sent = swap(partial_sums, 2)
        (result,) = attend_temporal(after(block, partial_sums))
        sent = after(sent, result)
        joined = call(
            functools.partial(merge_kernel, head_count, ((0,), (1,), (2,), (3,))),
            "merge",
            [(shard, width + lanes)] * 4,
            [],
            [kept, sent],
            flops=7 * 10**9,
        )
        pieces = [joined[0]] + [swap(joined[step], 4 * step) for step in (1, 2, 3)]
        text_keys = [keys_column, sent, swap(keys_column, 1), swap(sent, 1)]
    else:
        (result,) = attend_temporal(block)
        side = [[2 * chip + core for chip in range(devices // 2)] for core in range(2)]
        gathered = lax.all_gather(
            packed_text[:, :width], "frame", axis=0, tiled=True, axis_index_groups=side
        )
        partial_sums = lax.all_to_all(
            attend(gathered), "frame", 0, 0, tiled=True, axis_index_groups=side
        ).reshape(devices // 2, shard, width + lanes)
        blocks = [
            lambda head, i=i: partial_sums[i, :, head * lanes : (head + 1) * lanes]
            for i in range(devices // 2)
        ]
        _, total, factors = merge(head_count, blocks)
        text_out = jnp.concatenate(
            [
                weigh(head, factors, blocks) / total[:, head : head + 1]
                for head in range(head_count)
            ],
            axis=1,
        ).astype(jnp.bfloat16)
        all_keys = lax.all_gather(packed_text[:, width:], "frame", axis=0, tiled=True)
        text_keys = [all_keys]

    key_count = positions + devices * shard
    (spatial,) = call(
        functools.partial(spatial_kernel, head_count, shard, relative, scale),
        "spatial",
        [(positions, half * lanes)],
        [head_kind, text_len],
        [video, *text_keys],
        head_list + score_scratch(half, positions, key_count),
        flops=4 * positions * half * lanes * key_count,
    )
    if relative:
        pieces[0] = after(pieces[0], spatial)
        (text_out,) = call(
            functools.partial(finish_kernel, head_count), "finish",
            [(shard, width)],
            [],
            pieces,
            [pltpu.VMEM((shard, width), jnp.bfloat16), pltpu.SemaphoreType.DMA((2,))],
            out_space=pl.ANY,
        )
    temporal = lax.all_to_all(result, "frame", split_axis=0, concat_axis=0, tiled=True)
    (video_out,) = call(
        functools.partial(join_kernel, head_count),
        "join",
        [(positions, width)],
        [head_kind],
        [spatial, temporal],
        head_list,
    )
    return video_out.reshape(1, positions, width), text_out


def solution(mesh):
    in_specs = (
        P(None, ("groups", "frame"), None, None),
        P(None, ("groups", "frame"), None),
        P("groups"),
        P("groups"),
    )
    out_specs = (P(("groups", "frame"), None, None), P(("groups", "frame"), None))
    return jax.shard_map(
        functools.partial(body, mesh.shape["frame"]),
        mesh=mesh,
        in_specs=in_specs,
        out_specs=out_specs,
        check_vma=False,
    )
```

```python
import functools

import jax
import jax.numpy as jnp
from jax import lax
from jax.experimental import pallas as pl
from jax.experimental.pallas import tpu as pltpu
from jax.sharding import PartitionSpec as P

masked_score = -1e30
lanes = 128
stat_lanes = 32


def contract_last(a, b):
    return lax.dot_general(a, b, (((1,), (1,)), ((), ())), preferred_element_type=jnp.float32)


def head_lanes(head):
    if isinstance(head, int):
        return pl.ds(head * lanes, lanes)
    return pl.ds(pl.multiple_of(head * lanes, lanes), lanes)


def list_heads(kind_ref, list_ref, head_count):
    ones = jnp.int32(0)
    for head in range(head_count):
        kind = kind_ref[head]
        slot = jnp.where(kind == 1, head_count + ones, head - ones)
        list_ref[slot] = jnp.int32(head)
        ones = ones + kind


def pack_kernel(
    head_count,
    kind_ref,
    text_ref,
    video_ref,
    packed_ref,
    temporal_ref,
    list_ref,
    kind_here,
    text_here,
    video_here,
    packed_here,
    temporal_here,
    in_sems,
    out_sems,
):
    half = head_count // 2
    width = head_count * lanes
    copies = [
        pltpu.make_async_copy(kind_ref, kind_here, in_sems.at[0]),
        pltpu.make_async_copy(text_ref, text_here, in_sems.at[1]),
    ]
    for part in range(3):
        copies.append(
            pltpu.make_async_copy(video_ref.at[part], video_here.at[part], in_sems.at[part + 2])
        )
    for copy in copies:
        copy.start()
    copies[0].wait()
    list_heads(kind_here, list_ref, head_count)
    copies[1].wait()
    packed_here[:, :width] = text_here[0]
    for slot in range(half):
        for part in range(2):
            packed_here[:, head_lanes(head_count + part * half + slot)] = text_here[
                part + 1, :, head_lanes(list_ref[slot])
            ]
    sends = [pltpu.make_async_copy(packed_here, packed_ref, out_sems.at[0])]
    sends[0].start()
    for part in range(3):
        copies[part + 2].wait()
        for slot in range(half):
            temporal_here[:, head_lanes(part * half + slot)] = video_here[
                part, :, head_lanes(list_ref[head_count + slot])
            ]
        span = pl.ds(part * half * lanes, half * lanes)
        sends.append(
            pltpu.make_async_copy(
                temporal_here.at[:, span], temporal_ref.at[:, span], out_sems.at[part + 1]
            )
        )
        sends[-1].start()
    for send in sends:
        send.wait()


def stack_kernel(*refs):
    for half, out_ref in enumerate(refs[-2:]):
        width = out_ref.shape[1]
        out_ref[...] = jnp.concatenate(
            [ref[:, pl.ds(half * width, width)] for ref in refs[:-2]], axis=0
        )


def temporal_kernel(half, stride, scale, block_ref, out_ref, score_ref, weight_ref, here_ref, sems):
    rows = block_ref.shape[0]
    row = lax.broadcasted_iota(jnp.int32, (rows, rows), 0)
    column = lax.broadcasted_iota(jnp.int32, (rows, rows), 1)
    same = lax.rem(row, stride) == lax.rem(column, stride)
    for slot in range(half):
        score_ref[slot] = contract_last(
            block_ref[:, head_lanes(slot)], block_ref[:, head_lanes(half + slot)]
        )
    totals = []
    for slot in range(half):
        scores = jnp.where(same, score_ref[slot] * scale, masked_score)
        exps = jnp.exp(scores - scores.max(-1, keepdims=True))
        totals.append(exps.sum(-1, keepdims=True))
        weight_ref[slot] = exps.astype(jnp.bfloat16)
    sends = []
    for slot in range(half):
        summed = jnp.dot(
            weight_ref[slot],
            block_ref[:, head_lanes(2 * half + slot)],
            preferred_element_type=jnp.float32,
        )
        here_ref[:, head_lanes(slot)] = (summed / totals[slot]).astype(jnp.bfloat16)
        if slot % 2 == 1 or slot == half - 1:
            span = pl.ds((slot // 2) * 2 * lanes, (slot % 2 + 1) * lanes)
            sends.append(
                pltpu.make_async_copy(here_ref.at[:, span], out_ref.at[:, span], sems.at[slot // 2])
            )
            sends[-1].start()
    for send in sends:
        send.wait()


def spatial_kernel(
    head_count,
    shard,
    relative,
    scale,
    kind_ref,
    length_ref,
    video_ref,
    *refs,
):
    text_refs = refs[:-4]
    out_ref, list_ref, score_ref, weight_ref = refs[-4:]
    list_heads(kind_ref, list_ref, head_count)
    half = head_count // 2
    positions = video_ref.shape[1]
    text_total = sum(ref.shape[0] for ref in text_refs)
    index = lax.broadcasted_iota(jnp.int32, (8, text_total), 1)
    if relative:
        block = index // shard
        differs = (block & 3) * 4 + ((block >> 2) & 1) * 2 + ((block >> 3) & 1)
        index = (lax.axis_index("frame") ^ differs) * shard + lax.rem(index, shard)
    bias = jnp.where(index < length_ref[0], 0.0, masked_score)[:1]
    bias = jnp.concatenate([jnp.zeros((1, positions), jnp.float32), bias], axis=1)

    def gathered(part, slot):
        return jnp.concatenate(
            [video_ref[part + 1, :, head_lanes(list_ref[slot])]]
            + [
                ref[:, head_lanes(ref.shape[1] // lanes + (part - 2) * half + slot)]
                for ref in text_refs
            ],
            axis=0,
        )

    for slot in range(half):
        score_ref[slot] = contract_last(
            video_ref[0, :, head_lanes(list_ref[slot])], gathered(0, slot)
        )
    totals = []
    for slot in range(half):
        scores = score_ref[slot] * scale + bias
        exps = jnp.exp(scores - scores.max(-1, keepdims=True))
        totals.append(exps.sum(-1, keepdims=True))
        weight_ref[slot] = exps.astype(jnp.bfloat16)
    for slot in range(half):
        summed = jnp.dot(
            weight_ref[slot], gathered(1, slot), preferred_element_type=jnp.float32
        )
        out_ref[:, head_lanes(slot)] = (summed / totals[slot]).astype(jnp.bfloat16)


def text_kernel(head_count, shard, scale, length_ref, *refs):
    query_ref, key_refs, rider_refs = refs[0], refs[1:5], refs[5:-3]
    out_ref, score_ref, weight_ref = refs[-3:]
    rows = out_ref.shape[0]
    positions, text_rows = key_refs[0].shape[1], key_refs[2].shape[1]
    place = lax.broadcasted_iota(jnp.int32, (8, 2 * (positions + text_rows)), 1) - 2 * positions
    block = jnp.where(place >= text_rows, 1, 0)
    within = place - block * text_rows
    token = (lax.axis_index("frame") ^ block) * shard + within
    unused = (place >= 0) & ((within >= shard) | (token >= length_ref[0]))
    bias = jnp.where(unused, masked_score, 0.0)[:1]
    lane = lax.broadcasted_iota(jnp.int32, (rows, lanes), 1)
    stats = jnp.zeros((rows, lanes), jnp.float32)

    def gathered(part, head):
        return jnp.concatenate([ref[part, :, head_lanes(head)] for ref in key_refs], axis=0)

    for head in range(head_count):
        score_ref[head] = contract_last(query_ref[:, head_lanes(head)], gathered(1, head))
    for head in range(head_count):
        scores = score_ref[head] * scale + bias
        point = scores.max(-1, keepdims=True).astype(jnp.bfloat16).astype(jnp.float32)
        exps = jnp.exp(scores - point)
        total = exps.sum(-1, keepdims=True)
        weight_ref[head] = exps.astype(jnp.bfloat16)
        high = total.astype(jnp.bfloat16).astype(jnp.float32)
        for place, column in enumerate((point, high, total - high)):
            stats = jnp.where(lane == place * stat_lanes + head, column, stats)
    for head in range(head_count):
        summed = jnp.dot(
            weight_ref[head], gathered(2, head), preferred_element_type=jnp.float32
        )
        out_ref[:, head_lanes(head)] = summed.astype(jnp.bfloat16)
    out_ref[:, head_lanes(head_count)] = stats.astype(jnp.bfloat16)
    for ref in rider_refs:
        out_ref[:, pl.ds((head_count + 1) * lanes, ref.shape[1])] = ref[...]


def merge(head_count, blocks):
    stats = [block(head_count).astype(jnp.float32) for block in blocks]
    points, highs, lows = (
        [s[:, part * stat_lanes : (part + 1) * stat_lanes] for s in stats] for part in range(3)
    )
    point = functools.reduce(jnp.maximum, points)
    factors = [jnp.exp(p - point) for p in points]
    total = sum(f * (high + low) for f, high, low in zip(factors, highs, lows))
    return point, total, factors


def weigh(head, factors, blocks):
    return sum(
        f[:, head : head + 1] * block(head).astype(jnp.float32)
        for f, block in zip(factors, blocks)
    )


def reader(ref):
    return lambda head: ref[:, head_lanes(head)]


def merge_kernel(head_count, parts, first_ref, second_ref, *out_refs):
    blocks = [reader(first_ref), reader(second_ref)]
    point, total, factors = merge(head_count, blocks)
    high = total.astype(jnp.bfloat16).astype(jnp.float32)

    def store(head, merged):
        for ref, places in zip(out_refs, parts):
            ref[:, head_lanes(head)] = jnp.concatenate(
                [merged[i * 16 : (i + 1) * 16] for i in places], axis=0
            ).astype(jnp.bfloat16)

    for head in range(head_count):
        store(head, weigh(head, factors, blocks))
    store(head_count, jnp.concatenate([point, high, total - high, jnp.zeros_like(point)], axis=1))


def finish_kernel(head_count, *refs):
    out_ref, here_ref, sems = refs[-3:]
    blocks = [reader(ref) for ref in refs[:-3]]
    _, total, factors = merge(head_count, blocks)
    total = jnp.where(total > 0, total, 1.0)
    factors = [f / total for f in factors]
    half = head_count // 2
    sends = []
    for part in range(2):
        for head in range(part * half, (part + 1) * half):
            here_ref[:, head_lanes(head)] = weigh(head, factors, blocks).astype(jnp.bfloat16)
        span = pl.ds(part * half * lanes, half * lanes)
        sends.append(
            pltpu.make_async_copy(here_ref.at[:, span], out_ref.at[:, span], sems.at[part])
        )
        sends[-1].start()
    for send in sends:
        send.wait()


def join_kernel(head_count, kind_ref, spatial_ref, temporal_ref, out_ref, list_ref):
    list_heads(kind_ref, list_ref, head_count)
    half = head_count // 2
    for kind, ref in enumerate((spatial_ref, temporal_ref)):
        for slot in range(half):
            out_ref[:, head_lanes(list_ref[kind * head_count + slot])] = ref[
                :, pl.ds(slot * lanes, lanes)
            ]


def after(array, *others):
    return lax.optimization_barrier((array, *others))[0]


def after(array, *others):
    return lax.optimization_barrier((array, *others))[0]


def call(kernel, name, out, scalars, arrays, scratch=(), flops=0, space=pltpu.VMEM, out_space=pltpu.VMEM, limit=32):
    outs = [jax.ShapeDtypeStruct(shape, jnp.bfloat16) for shape in out]
    moved = sum(a.size * 2 for a in arrays) + sum(o.size * 2 for o in outs)
    return pl.pallas_call(
        kernel,
        out_shape=outs,
        in_specs=[pl.BlockSpec(memory_space=pltpu.SMEM)] * len(scalars)
        + [pl.BlockSpec(memory_space=space)] * len(arrays),
        out_specs=[pl.BlockSpec(memory_space=out_space)] * len(outs),
        scratch_shapes=scratch,
        compiler_params=pltpu.CompilerParams(vmem_limit_bytes=limit * 2**20),
        cost_estimate=pl.CostEstimate(flops=flops, bytes_accessed=moved, transcendentals=0),
        name=name,
    )(*scalars, *arrays)


def score_scratch(heads, rows, keys):
    return [pltpu.VMEM((heads, rows, keys), jnp.float32), pltpu.VMEM((heads, rows, keys), jnp.bfloat16)]


def body(devices, video_qkv, text_qkv, head_kind, text_len):
    head_count = head_kind.shape[0]
    half = head_count // 2
    width = video_qkv.shape[-1]
    positions = video_qkv.shape[2]
    shard = text_qkv.shape[1]
    scale = (width // head_count) ** -0.5
    video = video_qkv.reshape(3, positions, width)
    relative = devices == 16
    head_list = [pltpu.SMEM((2 * head_count,), jnp.int32)]

    def swap(array, bits):
        return lax.ppermute(array, "frame", [(i, i ^ bits) for i in range(devices)])

    packed_text, packed_video = call(
        functools.partial(pack_kernel, head_count),
        "pack",
        [(shard, 2 * width), (positions, 3 * half * lanes)],
        [],
        [head_kind, text_qkv, video],
        head_list
        + [pltpu.SMEM(head_kind.shape, jnp.int32)]
        + [pltpu.VMEM(a.shape, a.dtype) for a in (text_qkv, video)]
        + [pltpu.VMEM((shard, 2 * width), jnp.bfloat16)]
        + [pltpu.VMEM((positions, 3 * half * lanes), jnp.bfloat16)]
        + [pltpu.SemaphoreType.DMA((5,)), pltpu.SemaphoreType.DMA((4,))],
        space=pl.ANY,
        out_space=pl.ANY,
        limit=60,
    )
    block = lax.all_to_all(packed_video, "frame", split_axis=0, concat_axis=0, tiled=True)

    text_rows = -(-shard // 16) * 16
    text = jnp.pad(text_qkv, ((0, 0), (0, text_rows - shard), (0, 0)))
    other_text = swap(text, 1)
    keys = [video, swap(video, 1), text, other_text]

    def attend(queries, riders=()):
        rows = queries.shape[0]
        key_count = 2 * (positions + text_rows)
        return call(
            functools.partial(text_kernel, head_count, shard, scale),
            "text",
            [(rows, width + lanes + sum(r.shape[1] for r in riders))],
            [text_len],
            [queries, *keys, *riders],
            score_scratch(head_count, rows, key_count),
            flops=4 * rows * width * key_count,
        )[0]

    def attend_temporal(received):
        return call(
            functools.partial(temporal_kernel, half, positions // devices, scale),
            "temporal",
            [(positions, half * lanes)],
            [],
            [received],
            score_scratch(half, positions, positions)
            + [pltpu.VMEM((positions, half * lanes), jnp.bfloat16)]
            + [pltpu.SemaphoreType.DMA((-(-half // 2),))],
            flops=4 * positions * half * lanes * positions,
            out_space=pl.ANY,
        )

    if relative:
        column = [packed_text] + [swap(packed_text, 4 * step) for step in (1, 2, 3)]
        queries_column, keys_column = call(
            stack_kernel, "stack", [(4 * shard, width)] * 2, [], column, flops=8 * 10**9
        )
        across = swap(queries_column, 2)
        kept = attend(queries_column)
        across = after(across, kept)
        partial_sums = attend(across, [keys_column])
        sent = swap(partial_sums, 2)
        (result,) = attend_temporal(after(block, partial_sums))
        sent = after(sent, result)
        joined = call(
            functools.partial(merge_kernel, head_count, ((0,), (1,), (2,), (3,))),
            "merge",
            [(shard, width + lanes)] * 4,
            [],
            [kept, sent],
            flops=7 * 10**9,
        )
        pieces = [joined[0]] + [swap(joined[step], 4 * step) for step in (1, 2, 3)]
        text_keys = [keys_column, sent, swap(keys_column, 1), swap(sent[:, width + lanes :], 1)]
    else:
        (result,) = attend_temporal(block)
        side = [[2 * chip + core for chip in range(devices // 2)] for core in range(2)]
        gathered = lax.all_gather(
            packed_text[:, :width], "frame", axis=0, tiled=True, axis_index_groups=side
        )
        partial_sums = lax.all_to_all(
            attend(gathered), "frame", 0, 0, tiled=True, axis_index_groups=side
        ).reshape(devices // 2, shard, width + lanes)
        blocks = [
            lambda head, i=i: partial_sums[i, :, head * lanes : (head + 1) * lanes]
            for i in range(devices // 2)
        ]
        _, total, factors = merge(head_count, blocks)
        text_out = jnp.concatenate(
            [
                weigh(head, factors, blocks) / total[:, head : head + 1]
                for head in range(head_count)
            ],
            axis=1,
        ).astype(jnp.bfloat16)
        all_keys = lax.all_gather(packed_text[:, width:], "frame", axis=0, tiled=True)
        text_keys = [all_keys]

    key_count = positions + devices * shard
    (spatial,) = call(
        functools.partial(spatial_kernel, head_count, shard, relative, scale),
        "spatial",
        [(positions, half * lanes)],
        [head_kind, text_len],
        [video, *text_keys],
        head_list + score_scratch(half, positions, key_count),
        flops=4 * positions * half * lanes * key_count,
    )
    if relative:
        pieces[0] = after(pieces[0], spatial)
        (text_out,) = call(
            functools.partial(finish_kernel, head_count), "finish",
            [(shard, width)],
            [],
            pieces,
            [pltpu.VMEM((shard, width), jnp.bfloat16), pltpu.SemaphoreType.DMA((2,))],
            out_space=pl.ANY,
        )
    temporal = lax.all_to_all(result, "frame", split_axis=0, concat_axis=0, tiled=True)
    (video_out,) = call(
        functools.partial(join_kernel, head_count),
        "join",
        [(positions, width)],
        [head_kind],
        [spatial, temporal],
        head_list,
    )
    return video_out.reshape(1, positions, width), text_out


def solution(mesh):
    in_specs = (
        P(None, ("groups", "frame"), None, None),
        P(None, ("groups", "frame"), None),
        P("groups"),
        P("groups"),
    )
    out_specs = (P(("groups", "frame"), None, None), P(("groups", "frame"), None))
    return jax.shard_map(
        functools.partial(body, mesh.shape["frame"]),
        mesh=mesh,
        in_specs=in_specs,
        out_specs=out_specs,
        check_vma=False,
    )
```
